32 devices in a mesh: clips: 2 (over y), tm: 4 (over x, core), rows: 4 (over z).
Axes of the slice: x: 2, y: 2, z: 4, core: 2. Of those that a mesh axis runs over, the one named last changes fastest.
Arguments:
- segment_input: bfloat16 [4, 8, 4, 32, 384], P('clips', 'tm', 'rows'), parts along dimension 0, may hold values from -6 to 6
- inner_input: bfloat16 [4, 8, 4, 32, 384], P('clips', 'tm', 'rows'), parts along dimension 0, may hold values from -6 to 6
- lengths: int32 [4, 4], P('clips', 'tm'), parts along dimension 0, may hold values from 1 to 2
- inner_gain: float32 [384], replicated, may hold values from 0.25 to 1.75
- causal_weight: bfloat16 [3, 3, 3, 384, 384], replicated, may hold values from -0.0625 to 0.0625
- causal_bias: float32 [384], replicated, may hold values from -3 to 3
- attention_gain: float32 [384], replicated, may hold values from 0.25 to 1.75
- triple_weight: bfloat16 [384, 1152], replicated, may hold values from -0.4375 to 0.4375
- triple_bias: float32 [1152], replicated, may hold values from -150 to 150
- output_weight: bfloat16 [384, 384], replicated, may hold values from -0.3125 to 0.3125
- output_bias: float32 [384], replicated, may hold values from -3 to 3
Outputs:
- encoded: bfloat16 [4, 8, 4, 32, 384], P('clips', 'tm', 'rows'), parts along dimension 0
The draws below stay inside these ranges and needn't reach their ends.
There are 2 independent parts, one for each index of `clips`. The reference program is written for one: setup_inputs(seed, part) draws one part's arguments, and reference() takes and returns one part's arrays. A program takes and returns all parts, laid end to end along the dimension named above; an argument that names none is the same for every part. Nothing has to cross between parts.
Inputs may be any that keep to these rules, and one draw needn't show every extreme that they name: The valid frames of a clip in a section are that section's first lengths[b, s] frame slots.
All inputs are finite; a program needn't handle non-finite values.
Results may differ from the reference program's by a relative error of at most 0.0062.
Values may be sent and summed in bfloat16 or wider, within the bound.
A program may use at most 128 MiB of HBM per device.

```python
import math
import jax
import jax.numpy as jnp
from jax import lax

CH = 384
SEC_FRAMES = 2
COLS = 32
CLIPS = 2
FRAMES = 8
HEIGHT = 4
N_TM = 4


def draw_triple_bias(key, part):
    first_key = jax.random.fold_in(key, 11)
    return 0.5 * jax.random.truncated_normal(first_key, -6.0, 6.0, (3 * CH,), jnp.float32)


def with_ends(drawn, key, low, largest):
    shape = drawn.shape
    spot = [jax.random.randint(jax.random.fold_in(key, axis), (), 0, shape[axis]) for axis in range(len(shape))]
    drawn = drawn.at[tuple(spot)].set(low)
    longest = shape.index(max(shape))
    spot[longest] = (spot[longest] + 1) % shape[longest]
    return drawn.at[tuple(spot)].set(largest)


def block_levels(stream_key, extent, cuts, low, high):
    def one(dim, parts):
        heights = jax.random.uniform(jax.random.fold_in(jax.random.fold_in(stream_key, 6), dim), (parts,), jnp.float32, low / len(cuts), high / len(cuts))
        return jnp.repeat(jnp.exp(heights), extent[dim] // parts).reshape((-1,) + (1,) * (len(extent) - dim - 1))

    factor_of = one(*cuts[0])
    for cut in cuts[1:]:
        factor_of = factor_of * one(*cut)
    return factor_of


def bell_draw(rng, dims, spread, most, shards=(), held_as=jnp.bfloat16):
    entries = spread * jax.random.normal(rng, dims, jnp.float32)
    if shards:
        entries = entries * block_levels(rng, dims, shards, -0.22, 0.18)
    return jnp.clip(entries, -most, most).astype(held_as)


def setup_inputs(seed: int = 0, part: int = 0) -> dict:
    streams_of = jax.random.split(jax.random.key(seed), 12)
    part_keys = jax.random.split(jax.random.fold_in(streams_of[11], part), 12)
    segment_input = bell_draw(part_keys[0], (CLIPS, FRAMES, HEIGHT, COLS, CH), 1.0, 6.0, ((1, 4), (2, 4)))
    inner_input = bell_draw(part_keys[1], (CLIPS, FRAMES, HEIGHT, COLS, CH), 1.0, 6.0, ((1, 4), (2, 4)))
    lengths = with_ends(jax.random.randint(part_keys[2], (CLIPS, N_TM), 1, SEC_FRAMES + 1), jax.random.fold_in(part_keys[2], 1), 1, SEC_FRAMES).astype(jnp.int32)
    inner_gain = jnp.clip(1.0 + 0.15 * jax.random.normal(streams_of[3], (CH,), jnp.float32), 0.25, 1.75)
    causal_weight = bell_draw(streams_of[4], (3, 3, 3, CH, CH), (27 * CH) ** -0.5, 0.0625)
    causal_bias = bell_draw(streams_of[5], (CH,), 0.5, 3.0, (), jnp.float32)
    attention_gain = jnp.clip(1.0 + 0.15 * jax.random.normal(streams_of[6], (CH,), jnp.float32), 0.25, 1.75)
    triple_weight = bell_draw(streams_of[7], (CH, 3 * CH), (CH // 2) ** -0.5, 0.4375)
    triple_bias = draw_triple_bias(jax.random.fold_in(streams_of[11], 71), part)
    output_weight = bell_draw(streams_of[9], (CH, CH), CH ** -0.5, 0.3125)
    output_bias = bell_draw(streams_of[10], (CH,), 0.5, 3.0, (), jnp.float32)
    return dict(segment_input=segment_input, inner_input=inner_input, lengths=lengths, inner_gain=inner_gain, causal_weight=causal_weight, causal_bias=causal_bias, attention_gain=attention_gain, triple_weight=triple_weight, triple_bias=triple_bias, output_weight=output_weight, output_bias=output_bias)


EPSILON = 1e-06

def normalize(field, gain):
    widened = field.astype(jnp.float32)
    return widened * lax.rsqrt(lax.optimization_barrier(jnp.mean(widened * widened, axis=-1, keepdims=True)) + EPSILON) * gain

def last_two(extended, counts):
    slot_total = extended.shape[1]
    chosen = []
    for position in range(2):
        target = counts + position
        picked = jnp.zeros_like(extended[:, 0])
        for slot_index in range(slot_total):
            matches = (target == slot_index)[:, None, None, None]
            picked = jnp.where(matches, extended[:, slot_index], picked)
        chosen.append(picked)
    return jnp.stack(chosen, axis=1)

def convolve(padded, causal_weight, causal_bias):
    clip_count, slot_total, rows_padded, column_count, channels = padded.shape
    frame_count = slot_total - 2
    row_count = rows_padded - 2
    widened = jnp.pad(padded, ((0, 0), (0, 0), (0, 0), (1, 1), (0, 0)))
    summed = jnp.zeros((clip_count * frame_count * row_count * column_count, channels), jnp.float32)
    for delta_time in range(3):
        for delta_row in range(3):
            window = widened[:, delta_time:delta_time + frame_count, delta_row:delta_row + row_count]
            columns = jnp.concatenate([window[:, :, :, delta_col:delta_col + column_count] for delta_col in range(3)], axis=-1)
            kernel = causal_weight[delta_time, delta_row].reshape(3 * channels, channels)
            summed = summed + jnp.dot(columns.reshape(-1, 3 * channels), kernel, preferred_element_type=jnp.float32)
    return summed.reshape(clip_count, frame_count, row_count, column_count, channels) + causal_bias

def attend(normed, triple_weight, triple_bias, output_weight, output_bias):
    frame_count, places, channels = normed.shape
    packed = jnp.dot(normed.reshape(-1, channels), triple_weight, preferred_element_type=jnp.float32) + triple_bias
    packed = packed.reshape(frame_count, places, 3 * channels)
    queries = packed[:, :, :channels]
    key_vectors = packed[:, :, channels:2 * channels]
    values = packed[:, :, 2 * channels:].astype(jnp.bfloat16)
    scores = jnp.einsum('nqc,nkc->nqk', queries, key_vectors, precision=lax.Precision.HIGHEST) / math.sqrt(channels)
    row_max = lax.optimization_barrier(jnp.max(scores, axis=-1, keepdims=True))
    exponent = jnp.exp(scores - row_max)
    weights = (exponent / lax.optimization_barrier(jnp.sum(exponent, axis=-1, keepdims=True))).astype(jnp.bfloat16)
    weights, values = lax.optimization_barrier((weights, values))
    attended = jnp.einsum('nqk,nkc->nqc', weights.astype(jnp.float32), values.astype(jnp.float32), precision=lax.Precision.HIGHEST).astype(jnp.bfloat16)
    projected = jnp.dot(attended.reshape(-1, channels), output_weight, preferred_element_type=jnp.float32) + output_bias
    return projected.reshape(frame_count, places, channels).astype(jnp.bfloat16)

def reference(segment_input, inner_input, lengths, inner_gain, causal_weight, causal_bias, attention_gain, triple_weight, triple_bias, output_weight, output_bias):
    activated = jax.nn.silu(normalize(inner_input, inner_gain)).astype(jnp.bfloat16)
    clip_count = activated.shape[0]
    carried = jnp.zeros((clip_count, 2) + activated.shape[2:], jnp.bfloat16)
    outputs = []
    for section in range(N_TM):
        own_frames = activated[:, section * SEC_FRAMES:(section + 1) * SEC_FRAMES]
        extended = jnp.concatenate([carried, own_frames], axis=1)
        padded = jnp.pad(extended, ((0, 0), (0, 0), (1, 1), (0, 0), (0, 0)))
        outputs.append(convolve(padded, causal_weight, causal_bias))
        carried = last_two(extended, lengths[:, section].astype(jnp.int32))
    convolved = jnp.concatenate(outputs, axis=1)
    residual = (segment_input.astype(jnp.float32) + convolved).astype(jnp.bfloat16)
    residual = lax.optimization_barrier(residual)
    normed = normalize(residual, attention_gain).astype(jnp.bfloat16)
    clip_count, frame_count, height, column_count, channels = normed.shape
    blocks = normed.reshape(clip_count, frame_count, height * column_count, channels)
    projected = lax.map(lambda clip_block: attend(clip_block, triple_weight, triple_bias, output_weight, output_bias), blocks)
    projected = lax.optimization_barrier(projected.reshape(normed.shape))
    slot_index = jnp.arange(frame_count, dtype=jnp.int32)[None, :] % SEC_FRAMES
    live_mask = (slot_index < jnp.repeat(lengths.astype(jnp.int32), SEC_FRAMES, axis=1)).astype(jnp.float32)
    summed = (residual.astype(jnp.float32) + projected.astype(jnp.float32)) * live_mask[:, :, None, None, None]
    return summed.astype(jnp.bfloat16)
```

```python
import functools
import math

import jax
import jax.numpy as jnp
from jax import lax
from jax.experimental import pallas as pl
from jax.experimental.pallas import tpu as pltpu
from jax.sharding import PartitionSpec as P

EPSILON = 1e-06


def loop(count, step):
    if count == 1:
        step(0)
    else:

        def one(index, carry):
            step(index)
            return carry

        lax.fori_loop(0, count, one, 0)


TAPS = ((2, 1), (2, 0), (2, 2), (1, 1), (0, 1), (1, 0), (1, 2), (0, 0), (0, 2))
STAGES = ((0, 3), (3, 5), (5, 9))


def segment_kernel(
    n_tm,
    n_rows,
    clips,
    cols,
    ch,
    seg_ref,
    inner_ref,
    len_ref,
    inner_gain_ref,
    weight_ref,
    conv_bias_ref,
    attn_gain_ref,
    triple_ref,
    triple_bias_ref,
    output_ref,
    output_bias_ref,
    out_ref,
    ext,
    prev,
    prev2,
    last,
    flag_out,
    flag_in,
    wbuf,
    tbuf,
    obuf,
    conv,
    residual,
    normed,
    gathered,
    kbuf,
    vbuf,
    result,
    returned,
    wsem,
    psem,
    near_send,
    near_recv,
    tm_send,
    tm_recv,
    to_send,
    to_recv,
    back_send,
    back_recv,
):
    s = lax.axis_index("tm")
    r = lax.axis_index("rows")
    frames = 2 * clips
    per = frames // n_rows
    chunk = min(frames, 4)
    bf16, f32 = jnp.bfloat16, jnp.float32

    for i, (kt, kh) in enumerate(TAPS):
        for kw in range(3):
            pltpu.make_async_copy(
                weight_ref.at[kt, kh, kw],
                wbuf.at[pl.ds(i * ch, ch), pl.ds(kw * ch, ch)],
                wsem.at[i],
            ).start()
    triple_copy = pltpu.make_async_copy(triple_ref, tbuf, psem.at[0])
    output_copy = pltpu.make_async_copy(output_ref, obuf, psem.at[1])
    triple_copy.start()
    output_copy.start()

    barrier = pltpu.get_barrier_semaphore()
    for k in range(1, n_rows):
        pl.semaphore_signal(
            barrier,
            inc=1,
            device_id={"rows": lax.rem(r + k, n_rows)},
            device_id_type=pl.DeviceIdType.MESH,
        )
    expected = n_rows - 1
    for k in (-2, -1, 1, 2):
        there = jnp.logical_and(s + k >= 0, s + k < n_tm)
        expected = expected + there.astype(jnp.int32)

        @pl.when(there)
        def _():
            pl.semaphore_signal(
                barrier, inc=1, device_id={"tm": s + k}, device_id_type=pl.DeviceIdType.MESH
            )

    for b in range(clips):
        for t in range(2):
            field = inner_ref[b, t, 0].astype(f32)
            mean = jnp.mean(field * field, axis=-1, keepdims=True)
            v = field * lax.rsqrt(mean + EPSILON) * inner_gain_ref[...]
            ext[1, (2 + t) * clips + b] = (v / (1.0 + jnp.exp(-v))).astype(bf16)
        count = len_ref[b, 0]
        both = count == 2
        first = ext[1, 2 * clips + b].astype(f32)
        second = ext[1, 3 * clips + b].astype(f32)
        last[b] = jnp.where(both, second, first).astype(bf16)
        flag_out[b] = jnp.full((8, ch), count.astype(f32), f32)

    own = pl.ds(2 * clips, 2 * clips)
    cached = pl.ds(0, 2 * clips)
    blank = jnp.zeros((2 * clips, cols, ch), bf16)

    @pl.when(r == 0)
    def _():
        ext[0] = jnp.zeros((4 * clips, cols, ch), bf16)

    @pl.when(r == n_rows - 1)
    def _():
        ext[2] = jnp.zeros((4 * clips, cols, ch), bf16)

    @pl.when(s == 0)
    def _():
        ext[1, cached] = blank
        prev[...] = blank
        flag_in[...] = jnp.zeros((clips, 8, ch), f32)

        @pl.when(r > 0)
        def _():
            ext[0, cached] = blank

        @pl.when(r < n_rows - 1)
        def _():
            ext[2, cached] = blank

    @pl.when(s <= 1)
    def _():
        prev2[...] = jnp.zeros((clips, cols, ch), bf16)

    def remote(src, dst, send, recv, where):
        return pltpu.make_async_remote_copy(
            src_ref=src,
            dst_ref=dst,
            send_sem=send,
            recv_sem=recv,
            device_id=where,
            device_id_type=pl.DeviceIdType.MESH,
        )

    down, up = {"rows": r + 1}, {"rows": r - 1}
    has_down, has_up = r < n_rows - 1, r > 0
    own_down = remote(ext.at[1, own], ext.at[0, own], near_send.at[0], near_recv.at[0], down)
    own_up = remote(ext.at[1, own], ext.at[2, own], near_send.at[1], near_recv.at[1], up)
    old_down = remote(ext.at[1, cached], ext.at[0, cached], near_send.at[2], near_recv.at[2], down)
    old_up = remote(ext.at[1, cached], ext.at[2, cached], near_send.at[3], near_recv.at[3], up)
    to_next = remote(ext.at[1, own], prev, tm_send.at[0], tm_recv.at[0], {"tm": s + 1})
    to_flag = remote(flag_out, flag_in, tm_send.at[1], tm_recv.at[1], {"tm": s + 1})
    to_after = remote(last, prev2, tm_send.at[2], tm_recv.at[2], {"tm": s + 2})

    pl.semaphore_wait(barrier, expected)

    @pl.when(s + 1 < n_tm)
    def _():
        to_flag.start()
        to_next.start()

    @pl.when(s + 2 < n_tm)
    def _():
        to_after.start()

    @pl.when(has_down)
    def _():
        own_down.start()

    @pl.when(has_up)
    def _():
        own_up.start()

    @pl.when(s > 0)
    def _():
        to_flag.wait_recv()
        to_next.wait_recv()

        @pl.when(s > 1)
        def _():
            to_after.wait_recv()

        for b in range(clips):
            both = flag_in[b, 0:1, :] > 1.5
            first = prev[b].astype(f32)
            second = prev[clips + b].astype(f32)
            older = prev2[b].astype(f32)
            ext[1, clips + b] = jnp.where(both, second, first).astype(bf16)
            ext[1, b] = jnp.where(both, first, older).astype(bf16)

        @pl.when(has_down)
        def _():
            old_down.start()

        @pl.when(has_up)
        def _():
            old_up.start()

    def taps_dot(stage, at):
        begin, end = STAGES[stage]
        parts = [
            ext[kh, pl.ds(kt * clips + at * chunk, chunk)].reshape(chunk * cols, ch)
            for kt, kh in TAPS[begin:end]
        ]
        return jnp.dot(
            jnp.concatenate(parts, axis=-1),
            wbuf[begin * ch : end * ch, :],
            preferred_element_type=f32,
        )

    def weights_here(stage):
        for i in range(*STAGES[stage]):
            rows = wbuf.at[pl.ds(i * ch, ch)]
            pltpu.make_async_copy(rows, rows, wsem.at[i]).wait()

    @pl.when(has_up)
    def _():
        own_down.wait_recv()

    @pl.when(has_down)
    def _():
        own_up.wait_recv()

    weights_here(0)
    weights_here(1)

    def early(at):
        conv[at] = taps_dot(0, at) + taps_dot(1, at)

    loop(frames // chunk, early)
    weights_here(2)

    @pl.when(s > 0)
    def _():
        @pl.when(has_up)
        def _():
            old_down.wait_recv()

        @pl.when(has_down)
        def _():
            old_up.wait_recv()

    def late(at):
        total = conv[at] + taps_dot(2, at)
        places = chunk * cols
        column = lax.rem(lax.broadcasted_iota(jnp.int32, (places, ch), 0), cols)
        left = pltpu.roll(total[:, :ch], 1, 0)
        right = pltpu.roll(total[:, 2 * ch :], places - 1, 0)
        summed = total[:, ch : 2 * ch] + jnp.where(column == 0, 0.0, left)
        summed = summed + jnp.where(column == cols - 1, 0.0, right)
        summed = summed + conv_bias_ref[...]
        at_frames = pl.ds(at * chunk, chunk)
        held = residual[at_frames].reshape(places, ch).astype(f32)
        held = (held + summed).astype(bf16)
        residual[at_frames] = held.reshape(chunk, cols, ch)
        wide = held.astype(f32)
        mean = jnp.mean(wide * wide, axis=-1, keepdims=True)
        wide = (wide * lax.rsqrt(mean + EPSILON) * attn_gain_ref[...]).astype(bf16)
        normed[at_frames] = wide.reshape(chunk, cols, ch)

    for b in range(clips):
        for t in range(2):
            residual[t * clips + b] = seg_ref[b, t, 0]
    loop(frames // chunk, late)

    there = []
    for k in range(1, n_rows):
        peer = lax.rem(r + k, n_rows)
        copy = remote(
            normed.at[pl.ds(peer * per, per)],
            gathered.at[r],
            to_send.at[k - 1],
            to_recv.at[k - 1],
            {"rows": peer},
        )
        copy.start()
        there.append(copy)
    gathered[r] = normed[pl.ds(r * per, per)]
    triple_copy.wait()
    output_copy.wait()
    for copy in there:
        copy.wait_recv()

    groups = max(1, n_rows * cols // 128)
    height = n_rows // groups

    for frame in range(per):

        def project(at):
            x = gathered[pl.ds(at * height, height), frame].reshape(height * cols, ch)
            packed = jnp.dot(x, tbuf[:, ch:], preferred_element_type=f32)
            packed = packed + triple_bias_ref[:, ch:]
            rows = pl.ds(at * height * cols, height * cols)
            kbuf[rows] = packed[:, :ch]
            vbuf[rows] = packed[:, ch:].astype(bf16)

        def attend_rows(at):
            x = gathered[pl.ds(at * height, height), frame].reshape(height * cols, ch)
            queries = jnp.dot(x, tbuf[:, :ch], preferred_element_type=f32)
            queries = queries + triple_bias_ref[:, :ch]
            scores = lax.dot_general(
                queries,
                kbuf[...],
                (((1,), (1,)), ((), ())),
                precision=lax.Precision.HIGHEST,
                preferred_element_type=f32,
            ) / math.sqrt(ch)
            exponent = jnp.exp(scores - jnp.max(scores, axis=-1, keepdims=True))
            weights = (exponent / jnp.sum(exponent, axis=-1, keepdims=True)).astype(bf16)
            attended = jnp.dot(weights, vbuf[...], preferred_element_type=f32).astype(bf16)
            projected = jnp.dot(attended, obuf[...], preferred_element_type=f32)
            projected = (projected + output_bias_ref[...]).astype(bf16)
            result[pl.ds(at * height, height), frame] = projected.reshape(height, cols, ch)

        loop(groups, project)
        loop(groups, attend_rows)

    back = []
    for k in range(1, n_rows):
        peer = lax.rem(r + k, n_rows)
        copy = remote(
            result.at[peer],
            returned.at[pl.ds(r * per, per)],
            back_send.at[k - 1],
            back_recv.at[k - 1],
            {"rows": peer},
        )
        copy.start()
        back.append(copy)
    returned[pl.ds(r * per, per)] = result[r]
    for copy in back:
        copy.wait_recv()

    for b in range(clips):
        count = len_ref[b, 0]
        for t in range(2):
            f = t * clips + b
            live = (count > t).astype(f32)
            summed = residual[f].astype(f32) + returned[f].astype(f32)
            out_ref[b, t, 0] = (summed * live).astype(bf16)

    for copy in there + back:
        copy.wait_send()

    @pl.when(s + 1 < n_tm)
    def _():
        to_flag.wait_send()
        to_next.wait_send()

    @pl.when(s + 2 < n_tm)
    def _():
        to_after.wait_send()

    @pl.when(has_down)
    def _():
        own_down.wait_send()

    @pl.when(has_up)
    def _():
        own_up.wait_send()

    @pl.when(s > 0)
    def _():
        @pl.when(has_down)
        def _():
            old_down.wait_send()

        @pl.when(has_up)
        def _():
            old_up.wait_send()


def segment(
    n_tm,
    n_rows,
    segment_input,
    inner_input,
    lengths,
    inner_gain,
    causal_weight,
    causal_bias,
    attention_gain,
    triple_weight,
    triple_bias,
    output_weight,
    output_bias,
):
    clips, _, _, cols, ch = segment_input.shape
    frames = 2 * clips
    per = frames // n_rows
    chunk = min(frames, 4)
    bf16, f32 = jnp.bfloat16, jnp.float32
    vmem = pl.BlockSpec(memory_space=pltpu.VMEM)
    hbm = pl.BlockSpec(memory_space=pl.ANY)
    smem = pl.BlockSpec(memory_space=pltpu.SMEM)
    dma = pltpu.SemaphoreType.DMA
    return pl.pallas_call(
        functools.partial(segment_kernel, n_tm, n_rows, clips, cols, ch),
        out_shape=jax.ShapeDtypeStruct(segment_input.shape, bf16),
        in_specs=[vmem, vmem, smem, vmem, hbm, vmem, vmem, hbm, vmem, hbm, vmem],
        out_specs=vmem,
        scratch_shapes=[
            pltpu.VMEM((3, 4 * clips, cols, ch), bf16),
            pltpu.VMEM((2 * clips, cols, ch), bf16),
            pltpu.VMEM((clips, cols, ch), bf16),
            pltpu.VMEM((clips, cols, ch), bf16),
            pltpu.VMEM((clips, 8, ch), f32),
            pltpu.VMEM((clips, 8, ch), f32),
            pltpu.VMEM((9 * ch, 3 * ch), bf16),
            pltpu.VMEM((ch, 3 * ch), bf16),
            pltpu.VMEM((ch, ch), bf16),
            pltpu.VMEM((frames // chunk, chunk * cols, 3 * ch), f32),
            pltpu.VMEM((frames, cols, ch), bf16),
            pltpu.VMEM((frames, cols, ch), bf16),
            pltpu.VMEM((n_rows, per, cols, ch), bf16),
            pltpu.VMEM((n_rows * cols, ch), f32),
            pltpu.VMEM((n_rows * cols, ch), bf16),
            pltpu.VMEM((n_rows, per, cols, ch), bf16),
            pltpu.VMEM((frames, cols, ch), bf16),
            dma((9,)),
            dma((2,)),
            dma((4,)),
            dma((4,)),
            dma((3,)),
            dma((3,)),
            dma((n_rows - 1,)),
            dma((n_rows - 1,)),
            dma((n_rows - 1,)),
            dma((n_rows - 1,)),
        ],
        compiler_params=pltpu.CompilerParams(
            collective_id=0, has_side_effects=True, vmem_limit_bytes=56 * 1024 * 1024
        ),
        name="segment",
    )(
        segment_input,
        inner_input,
        lengths,
        inner_gain[None],
        causal_weight,
        causal_bias[None],
        attention_gain[None],
        triple_weight,
        triple_bias[None],
        output_weight,
        output_bias[None],
    )


def solution(mesh):
    placed = (
        P("clips", "tm", "rows", None, None),
        P("clips", "tm", "rows", None, None),
        P("clips", "tm"),
        P(),
        P(),
        P(),
        P(),
        P(),
        P(),
        P(),
        P(),
    )
    return jax.shard_map(
        functools.partial(segment, mesh.shape["tm"], mesh.shape["rows"]),
        mesh=mesh,
        in_specs=placed,
        out_specs=P("clips", "tm", "rows", None, None),
        check_vma=False,
    )
```

```python
import functools
import math

import jax
import jax.numpy as jnp
from jax import lax
from jax.experimental import pallas as pl
from jax.experimental.pallas import tpu as pltpu
from jax.sharding import PartitionSpec as P

EPSILON = 1e-06


def loop(count, step):
    if count == 1:
        step(0)
    else:

        def one(index, carry):
            step(index)
            return carry

        lax.fori_loop(0, count, one, 0)


TAPS = ((2, 1), (2, 0), (2, 2), (1, 1), (0, 1), (1, 0), (1, 2), (0, 0), (0, 2))
STAGES = ((0, 3), (3, 5), (5, 9))


def segment_kernel(
    n_tm,
    n_rows,
    clips,
    cols,
    ch,
    seg_any,
    inner_any,
    len_any,
    inner_gain_any,
    weight_ref,
    conv_bias_any,
    attn_gain_any,
    triple_ref,
    triple_bias_any,
    output_ref,
    output_bias_any,
    out_ref,
    seg_ref,
    inner_ref,
    len_ref,
    inner_gain_ref,
    conv_bias_ref,
    attn_gain_ref,
    triple_bias_ref,
    output_bias_ref,
    insem,
    ext,
    prev,
    prev2,
    last,
    flag_out,
    flag_in,
    wbuf,
    tbuf,
    obuf,
    conv,
    residual,
    normed,
    gathered,
    kbuf,
    vbuf,
    result,
    returned,
    wsem,
    psem,
    near_send,
    near_recv,
    tm_send,
    tm_recv,
    to_send,
    to_recv,
    back_send,
    back_recv,
):
    s = lax.axis_index("tm")
    r = lax.axis_index("rows")
    frames = 2 * clips
    per = frames // n_rows
    chunk = min(frames, 4)
    bf16, f32 = jnp.bfloat16, jnp.float32

    barrier = pltpu.get_barrier_semaphore()
    for k in range(1, n_rows):
        pl.semaphore_signal(
            barrier,
            inc=1,
            device_id={"rows": lax.rem(r + k, n_rows)},
            device_id_type=pl.DeviceIdType.MESH,
        )
    expected = n_rows - 1
    for k in (-2, -1, 1, 2):
        there = jnp.logical_and(s + k >= 0, s + k < n_tm)
        expected = expected + there.astype(jnp.int32)

        @pl.when(there)
        def _():
            pl.semaphore_signal(
                barrier, inc=1, device_id={"tm": s + k}, device_id_type=pl.DeviceIdType.MESH
            )

    small = [
        pltpu.make_async_copy(src, dst, insem.at[i])
        for i, (src, dst) in enumerate(
            (
                (inner_any, inner_ref),
                (inner_gain_any, inner_gain_ref),
                (len_any, len_ref),
                (seg_any, seg_ref),
                (conv_bias_any, conv_bias_ref),
                (attn_gain_any, attn_gain_ref),
                (triple_bias_any, triple_bias_ref),
                (output_bias_any, output_bias_ref),
            )
        )
    ]
    for copy in small:
        copy.start()

    for i, (kt, kh) in enumerate(TAPS):
        for kw in range(3):
            pltpu.make_async_copy(
                weight_ref.at[kt, kh, kw],
                wbuf.at[pl.ds(i * ch, ch), pl.ds(kw * ch, ch)],
                wsem.at[i],
            ).start()
    triple_copy = pltpu.make_async_copy(triple_ref, tbuf, psem.at[0])
    output_copy = pltpu.make_async_copy(output_ref, obuf, psem.at[1])
    triple_copy.start()
    output_copy.start()

    for copy in small[:3]:
        copy.wait()
    inner_gain = inner_gain_ref[...].reshape(1, ch)

    for b in range(clips):
        for t in range(2):
            field = inner_ref[b, t, 0].astype(f32)
            mean = jnp.mean(field * field, axis=-1, keepdims=True)
            v = field * lax.rsqrt(mean + EPSILON) * inner_gain
            ext[1, (2 + t) * clips + b] = (v / (1.0 + jnp.exp(-v))).astype(bf16)
        count = len_ref[0, b]
        both = count == 2
        first = ext[1, 2 * clips + b].astype(f32)
        second = ext[1, 3 * clips + b].astype(f32)
        last[b] = jnp.where(both, second, first).astype(bf16)
        flag_out[b] = jnp.full((8, ch), count.astype(f32), f32)

    own = pl.ds(2 * clips, 2 * clips)
    cached = pl.ds(0, 2 * clips)
    blank = jnp.zeros((2 * clips, cols, ch), bf16)

    @pl.when(r == 0)
    def _():
        ext[0] = jnp.zeros((4 * clips, cols, ch), bf16)

    @pl.when(r == n_rows - 1)
    def _():
        ext[2] = jnp.zeros((4 * clips, cols, ch), bf16)

    @pl.when(s == 0)
    def _():
        ext[1, cached] = blank
        prev[...] = blank
        flag_in[...] = jnp.zeros((clips, 8, ch), f32)

        @pl.when(r > 0)
        def _():
            ext[0, cached] = blank

        @pl.when(r < n_rows - 1)
        def _():
            ext[2, cached] = blank

    @pl.when(s <= 1)
    def _():
        prev2[...] = jnp.zeros((clips, cols, ch), bf16)

    def remote(src, dst, send, recv, where):
        return pltpu.make_async_remote_copy(
            src_ref=src,
            dst_ref=dst,
            send_sem=send,
            recv_sem=recv,
            device_id=where,
            device_id_type=pl.DeviceIdType.MESH,
        )

    down, up = {"rows": r + 1}, {"rows": r - 1}
    has_down, has_up = r < n_rows - 1, r > 0
    own_down = remote(ext.at[1, own], ext.at[0, own], near_send.at[0], near_recv.at[0], down)
    own_up = remote(ext.at[1, own], ext.at[2, own], near_send.at[1], near_recv.at[1], up)
    old_down = remote(ext.at[1, cached], ext.at[0, cached], near_send.at[2], near_recv.at[2], down)
    old_up = remote(ext.at[1, cached], ext.at[2, cached], near_send.at[3], near_recv.at[3], up)
    to_next = remote(ext.at[1, own], prev, tm_send.at[0], tm_recv.at[0], {"tm": s + 1})
    to_flag = remote(flag_out, flag_in, tm_send.at[1], tm_recv.at[1], {"tm": s + 1})
    to_after = remote(last, prev2, tm_send.at[2], tm_recv.at[2], {"tm": s + 2})

    pl.semaphore_wait(barrier, expected)

    @pl.when(s + 1 < n_tm)
    def _():
        to_flag.start()
        to_next.start()

    @pl.when(s + 2 < n_tm)
    def _():
        to_after.start()

    @pl.when(has_down)
    def _():
        own_down.start()

    @pl.when(has_up)
    def _():
        own_up.start()

    @pl.when(s > 0)
    def _():
        to_flag.wait_recv()
        to_next.wait_recv()

        @pl.when(s > 1)
        def _():
            to_after.wait_recv()

        for b in range(clips):
            both = flag_in[b, 0:1, :] > 1.5
            first = prev[b].astype(f32)
            second = prev[clips + b].astype(f32)
            older = prev2[b].astype(f32)
            ext[1, clips + b] = jnp.where(both, second, first).astype(bf16)
            ext[1, b] = jnp.where(both, first, older).astype(bf16)

        @pl.when(has_down)
        def _():
            old_down.start()

        @pl.when(has_up)
        def _():
            old_up.start()

    def taps_dot(stage, at):
        begin, end = STAGES[stage]
        parts = [
            ext[kh, pl.ds(kt * clips + at * chunk, chunk)].reshape(chunk * cols, ch)
            for kt, kh in TAPS[begin:end]
        ]
        return jnp.dot(
            jnp.concatenate(parts, axis=-1),
            wbuf[begin * ch : end * ch, :],
            preferred_element_type=f32,
        )

    def weights_here(stage):
        for i in range(*STAGES[stage]):
            rows = wbuf.at[pl.ds(i * ch, ch)]
            pltpu.make_async_copy(rows, rows, wsem.at[i]).wait()

    @pl.when(has_up)
    def _():
        own_down.wait_recv()

    @pl.when(has_down)
    def _():
        own_up.wait_recv()

    weights_here(0)
    weights_here(1)

    def early(at):
        conv[at] = taps_dot(0, at) + taps_dot(1, at)

    loop(frames // chunk, early)
    weights_here(2)

    @pl.when(s > 0)
    def _():
        @pl.when(has_up)
        def _():
            old_down.wait_recv()

        @pl.when(has_down)
        def _():
            old_up.wait_recv()

    for copy in small[3:]:
        copy.wait()
    conv_bias = conv_bias_ref[...].reshape(1, ch)
    attn_gain = attn_gain_ref[...].reshape(1, ch)
    triple_bias = triple_bias_ref[...].reshape(1, 3 * ch)
    output_bias = output_bias_ref[...].reshape(1, ch)

    def late(at):
        total = conv[at] + taps_dot(2, at)
        places = chunk * cols
        column = lax.rem(lax.broadcasted_iota(jnp.int32, (places, ch), 0), cols)
        left = pltpu.roll(total[:, :ch], 1, 0)
        right = pltpu.roll(total[:, 2 * ch :], places - 1, 0)
        summed = total[:, ch : 2 * ch] + jnp.where(column == 0, 0.0, left)
        summed = summed + jnp.where(column == cols - 1, 0.0, right)
        summed = summed + conv_bias
        at_frames = pl.ds(at * chunk, chunk)
        held = residual[at_frames].reshape(places, ch).astype(f32)
        held = (held + summed).astype(bf16)
        residual[at_frames] = held.reshape(chunk, cols, ch)
        wide = held.astype(f32)
        mean = jnp.mean(wide * wide, axis=-1, keepdims=True)
        wide = (wide * lax.rsqrt(mean + EPSILON) * attn_gain).astype(bf16)
        normed[at_frames] = wide.reshape(chunk, cols, ch)

    for b in range(clips):
        for t in range(2):
            residual[t * clips + b] = seg_ref[b, t, 0]
    loop(frames // chunk, late)

    there = []
    for k in range(1, n_rows):
        peer = lax.rem(r + k, n_rows)
        copy = remote(
            normed.at[pl.ds(peer * per, per)],
            gathered.at[r],
            to_send.at[k - 1],
            to_recv.at[k - 1],
            {"rows": peer},
        )
        copy.start()
        there.append(copy)
    gathered[r] = normed[pl.ds(r * per, per)]
    triple_copy.wait()
    output_copy.wait()
    for copy in there:
        copy.wait_recv()

    groups = max(1, n_rows * cols // 128)
    height = n_rows // groups

    for frame in range(per):

        def project(at):
            x = gathered[pl.ds(at * height, height), frame].reshape(height * cols, ch)
            packed = jnp.dot(x, tbuf[:, ch:], preferred_element_type=f32)
            packed = packed + triple_bias[:, ch:]
            rows = pl.ds(at * height * cols, height * cols)
            kbuf[rows] = packed[:, :ch]
            vbuf[rows] = packed[:, ch:].astype(bf16)

        def attend_rows(at):
            x = gathered[pl.ds(at * height, height), frame].reshape(height * cols, ch)
            queries = jnp.dot(x, tbuf[:, :ch], preferred_element_type=f32)
            queries = queries + triple_bias[:, :ch]
            scores = lax.dot_general(
                queries,
                kbuf[...],
                (((1,), (1,)), ((), ())),
                precision=lax.Precision.HIGHEST,
                preferred_element_type=f32,
            ) / math.sqrt(ch)
            exponent = jnp.exp(scores - jnp.max(scores, axis=-1, keepdims=True))
            weights = (exponent / jnp.sum(exponent, axis=-1, keepdims=True)).astype(bf16)
            attended = jnp.dot(weights, vbuf[...], preferred_element_type=f32).astype(bf16)
            projected = jnp.dot(attended, obuf[...], preferred_element_type=f32)
            projected = (projected + output_bias).astype(bf16)
            result[pl.ds(at * height, height), frame] = projected.reshape(height, cols, ch)

        loop(groups, project)
        loop(groups, attend_rows)

    back = []
    for k in range(1, n_rows):
        peer = lax.rem(r + k, n_rows)
        copy = remote(
            result.at[peer],
            returned.at[pl.ds(r * per, per)],
            back_send.at[k - 1],
            back_recv.at[k - 1],
            {"rows": peer},
        )
        copy.start()
        back.append(copy)
    returned[pl.ds(r * per, per)] = result[r]
    for copy in back:
        copy.wait_recv()

    for b in range(clips):
        count = len_ref[0, b]
        for t in range(2):
            f = t * clips + b
            live = (count > t).astype(f32)
            summed = residual[f].astype(f32) + returned[f].astype(f32)
            out_ref[b, t, 0] = (summed * live).astype(bf16)

    for copy in there + back:
        copy.wait_send()

    @pl.when(s + 1 < n_tm)
    def _():
        to_flag.wait_send()
        to_next.wait_send()

    @pl.when(s + 2 < n_tm)
    def _():
        to_after.wait_send()

    @pl.when(has_down)
    def _():
        own_down.wait_send()

    @pl.when(has_up)
    def _():
        own_up.wait_send()

    @pl.when(s > 0)
    def _():
        @pl.when(has_down)
        def _():
            old_down.wait_send()

        @pl.when(has_up)
        def _():
            old_up.wait_send()


def segment(
    n_tm,
    n_rows,
    segment_input,
    inner_input,
    lengths,
    inner_gain,
    causal_weight,
    causal_bias,
    attention_gain,
    triple_weight,
    triple_bias,
    output_weight,
    output_bias,
):
    clips, _, _, cols, ch = segment_input.shape
    frames = 2 * clips
    per = frames // n_rows
    chunk = min(frames, 4)
    bf16, f32 = jnp.bfloat16, jnp.float32
    vmem = pl.BlockSpec(memory_space=pltpu.VMEM)
    hbm = pl.BlockSpec(memory_space=pl.ANY)
    dma = pltpu.SemaphoreType.DMA
    return pl.pallas_call(
        functools.partial(segment_kernel, n_tm, n_rows, clips, cols, ch),
        out_shape=jax.ShapeDtypeStruct(segment_input.shape, bf16),
        in_specs=[hbm] * 11,
        out_specs=vmem,
        scratch_shapes=[
            pltpu.VMEM(segment_input.shape, bf16),
            pltpu.VMEM(inner_input.shape, bf16),
            pltpu.SMEM((1, clips), jnp.int32),
            pltpu.VMEM((ch,), f32),
            pltpu.VMEM((ch,), f32),
            pltpu.VMEM((ch,), f32),
            pltpu.VMEM((3 * ch,), f32),
            pltpu.VMEM((ch,), f32),
            dma((8,)),
            pltpu.VMEM((3, 4 * clips, cols, ch), bf16),
            pltpu.VMEM((2 * clips, cols, ch), bf16),
            pltpu.VMEM((clips, cols, ch), bf16),
            pltpu.VMEM((clips, cols, ch), bf16),
            pltpu.VMEM((clips, 8, ch), f32),
            pltpu.VMEM((clips, 8, ch), f32),
            pltpu.VMEM((9 * ch, 3 * ch), bf16),
            pltpu.VMEM((ch, 3 * ch), bf16),
            pltpu.VMEM((ch, ch), bf16),
            pltpu.VMEM((frames // chunk, chunk * cols, 3 * ch), f32),
            pltpu.VMEM((frames, cols, ch), bf16),
            pltpu.VMEM((frames, cols, ch), bf16),
            pltpu.VMEM((n_rows, per, cols, ch), bf16),
            pltpu.VMEM((n_rows * cols, ch), f32),
            pltpu.VMEM((n_rows * cols, ch), bf16),
            pltpu.VMEM((n_rows, per, cols, ch), bf16),
            pltpu.VMEM((frames, cols, ch), bf16),
            dma((9,)),
            dma((2,)),
            dma((4,)),
            dma((4,)),
            dma((3,)),
            dma((3,)),
            dma((n_rows - 1,)),
            dma((n_rows - 1,)),
            dma((n_rows - 1,)),
            dma((n_rows - 1,)),
        ],
        compiler_params=pltpu.CompilerParams(
            collective_id=0, has_side_effects=True, vmem_limit_bytes=56 * 1024 * 1024
        ),
        name="segment",
    )(
        segment_input,
        inner_input,
        lengths.T,
        inner_gain,
        causal_weight,
        causal_bias,
        attention_gain,
        triple_weight,
        triple_bias,
        output_weight,
        output_bias,
    )


def solution(mesh):
    placed = (
        P("clips", "tm", "rows", None, None),
        P("clips", "tm", "rows", None, None),
        P("clips", "tm"),
        P(),
        P(),
        P(),
        P(),
        P(),
        P(),
        P(),
        P(),
    )
    return jax.shard_map(
        functools.partial(segment, mesh.shape["tm"], mesh.shape["rows"]),
        mesh=mesh,
        in_specs=placed,
        out_specs=P("clips", "tm", "rows", None, None),
        check_vma=False,
    )
```

```python
import functools
import math

import jax
import jax.numpy as jnp
from jax import lax
from jax.experimental import pallas as pl
from jax.experimental.pallas import tpu as pltpu
from jax.sharding import PartitionSpec as P

EPSILON = 1e-06


def loop(count, step):
    if count == 1:
        step(0)
    else:

        def one(index, carry):
            step(index)
            return carry

        lax.fori_loop(0, count, one, 0)


TAPS = ((2, 1), (1, 1), (0, 1), (2, 0), (2, 2), (1, 0), (1, 2), (0, 0), (0, 2))
STAGES = ((0, 1), (1, 3), (3, 5), (5, 9))


def segment_kernel(
    n_tm,
    n_rows,
    clips,
    cols,
    ch,
    seg_any,
    inner_any,
    len_any,
    inner_gain_any,
    weight_ref,
    conv_bias_any,
    attn_gain_any,
    triple_ref,
    triple_bias_any,
    output_ref,
    output_bias_any,
    out_ref,
    seg_ref,
    inner_ref,
    len_ref,
    inner_gain_ref,
    conv_bias_ref,
    attn_gain_ref,
    triple_bias_ref,
    output_bias_ref,
    insem,
    ext,
    prev,
    prev2,
    last,
    flag_out,
    flag_in,
    wbuf,
    tbuf,
    obuf,
    conv,
    residual,
    normed,
    gathered,
    kbuf,
    vbuf,
    result,
    returned,
    wsem,
    psem,
    near_send,
    near_recv,
    tm_send,
    tm_recv,
    to_send,
    to_recv,
    back_send,
    back_recv,
):
    s = lax.axis_index("tm")
    r = lax.axis_index("rows")
    frames = 2 * clips
    per = frames // n_rows
    chunk = 2 - clips % 2
    places = 2 * chunk * cols
    halves = 2 if clips % 2 == 0 else 1
    share = clips // halves
    bf16, f32 = jnp.bfloat16, jnp.float32

    barrier = pltpu.get_barrier_semaphore()
    for k in range(1, n_rows):
        pl.semaphore_signal(
            barrier,
            inc=1,
            device_id={"rows": lax.rem(r + k, n_rows)},
            device_id_type=pl.DeviceIdType.MESH,
        )
    expected = n_rows - 1
    for k in (-2, -1, 1, 2):
        there = jnp.logical_and(s + k >= 0, s + k < n_tm)
        expected = expected + there.astype(jnp.int32)

        @pl.when(there)
        def _():
            pl.semaphore_signal(
                barrier, inc=1, device_id={"tm": s + k}, device_id_type=pl.DeviceIdType.MESH
            )

    small = [
        pltpu.make_async_copy(src, dst, insem.at[i])
        for i, (src, dst) in enumerate(
            (
                (inner_any, inner_ref),
                (inner_gain_any, inner_gain_ref),
                (len_any, len_ref),
                (seg_any, seg_ref),
                (conv_bias_any, conv_bias_ref),
                (attn_gain_any, attn_gain_ref),
                (triple_bias_any, triple_bias_ref),
                (output_bias_any, output_bias_ref),
            )
        )
    ]
    for copy in small:
        copy.start()

    for i, (kt, kh) in enumerate(TAPS):
        for kw in range(3):
            pltpu.make_async_copy(
                weight_ref.at[kt, kh, kw],
                wbuf.at[pl.ds(i * ch, ch), pl.ds(kw * ch, ch)],
                wsem.at[i],
            ).start()
    triple_copy = pltpu.make_async_copy(triple_ref, tbuf, psem.at[0])
    output_copy = pltpu.make_async_copy(output_ref, obuf, psem.at[1])
    triple_copy.start()
    output_copy.start()

    for copy in small[:3]:
        copy.wait()
    inner_gain = inner_gain_ref[...].reshape(1, ch)

    for b in range(clips):
        for t in range(2):
            field = inner_ref[b, t, 0].astype(f32)
            mean = jnp.mean(field * field, axis=-1, keepdims=True)
            v = field * lax.rsqrt(mean + EPSILON) * inner_gain
            ext[1, b, 2 + t] = (v / (1.0 + jnp.exp(-v))).astype(bf16)
        count = len_ref[0, b]
        both = count == 2
        first = ext[1, b, 2].astype(f32)
        second = ext[1, b, 3].astype(f32)
        last[b] = jnp.where(both, second, first).astype(bf16)
        flag_out[b] = jnp.full((8, ch), count.astype(f32), f32)

    own, cached = pl.ds(2, 2), pl.ds(0, 2)
    blank = jnp.zeros((clips, 2, cols, ch), bf16)

    @pl.when(r == 0)
    def _():
        ext[0] = jnp.zeros((clips, 4, cols, ch), bf16)

    @pl.when(r == n_rows - 1)
    def _():
        ext[2] = jnp.zeros((clips, 4, cols, ch), bf16)

    @pl.when(s == 0)
    def _():
        ext[1, :, cached] = blank
        prev[...] = blank
        flag_in[...] = jnp.zeros((clips, 8, ch), f32)

        @pl.when(r > 0)
        def _():
            ext[0, :, cached] = blank

        @pl.when(r < n_rows - 1)
        def _():
            ext[2, :, cached] = blank

    @pl.when(s <= 1)
    def _():
        prev2[...] = jnp.zeros((clips, cols, ch), bf16)

    def remote(src, dst, send, recv, where):
        return pltpu.make_async_remote_copy(
            src_ref=src,
            dst_ref=dst,
            send_sem=send,
            recv_sem=recv,
            device_id=where,
            device_id_type=pl.DeviceIdType.MESH,
        )

    down, up = {"rows": r + 1}, {"rows": r - 1}
    has_down, has_up = r < n_rows - 1, r > 0
    own_down = remote(ext.at[1, :, own], ext.at[0, :, own], near_send.at[0], near_recv.at[0], down)
    own_up = remote(ext.at[1, :, own], ext.at[2, :, own], near_send.at[1], near_recv.at[1], up)
    to_flag = remote(flag_out, flag_in, tm_send.at[0], tm_recv.at[0], {"tm": s + 1})
    old_down, old_up, to_next, to_after = [], [], [], []
    for g in range(halves):
        part = pl.ds(g * share, share)
        mine = ext.at[1, part, cached]
        i, j = 2 + 2 * g, 3 + 2 * g
        old_down.append(
            remote(mine, ext.at[0, part, cached], near_send.at[i], near_recv.at[i], down)
        )
        old_up.append(remote(mine, ext.at[2, part, cached], near_send.at[j], near_recv.at[j], up))
        i, j = 1 + 2 * g, 2 + 2 * g
        to_next.append(
            remote(
                ext.at[1, part, own], prev.at[part], tm_send.at[i], tm_recv.at[i], {"tm": s + 1}
            )
        )
        to_after.append(
            remote(last.at[part], prev2.at[part], tm_send.at[j], tm_recv.at[j], {"tm": s + 2})
        )

    pl.semaphore_wait(barrier, expected)

    @pl.when(s + 1 < n_tm)
    def _():
        to_flag.start()

    for g in range(halves):

        @pl.when(s + 1 < n_tm)
        def _():
            to_next[g].start()

        @pl.when(s + 2 < n_tm)
        def _():
            to_after[g].start()

    @pl.when(has_down)
    def _():
        own_down.start()

    @pl.when(has_up)
    def _():
        own_up.start()

    def taps_dot(stage, at):
        begin, end = STAGES[stage]
        parts = [
            ext[kh, pl.ds(at * chunk, chunk), kt : kt + 2].reshape(places, ch)
            for kt, kh in TAPS[begin:end]
        ]
        return jnp.dot(
            jnp.concatenate(parts, axis=-1),
            wbuf[begin * ch : end * ch, :],
            preferred_element_type=f32,
        )

    def weights_here(stage):
        for i in range(*STAGES[stage]):
            rows = wbuf.at[pl.ds(i * ch, ch)]
            pltpu.make_async_copy(rows, rows, wsem.at[i]).wait()

    def start(at):
        conv[at] = taps_dot(0, at)

    weights_here(0)
    loop(clips // chunk, start)

    @pl.when(s > 0)
    def _():
        to_flag.wait_recv()
        for g in range(halves):
            to_next[g].wait_recv()

            @pl.when(s > 1)
            def _():
                to_after[g].wait_recv()

            for b in range(g * share, (g + 1) * share):
                both = flag_in[b, 0:1, :] > 1.5
                first = prev[b, 0].astype(f32)
                second = prev[b, 1].astype(f32)
                older = prev2[b].astype(f32)
                ext[1, b, 1] = jnp.where(both, second, first).astype(bf16)
                ext[1, b, 0] = jnp.where(both, first, older).astype(bf16)

            @pl.when(has_down)
            def _():
                old_down[g].start()

            @pl.when(has_up)
            def _():
                old_up[g].start()

    weights_here(1)

    def center(at):
        conv[at] += taps_dot(1, at)

    loop(clips // chunk, center)

    @pl.when(has_up)
    def _():
        own_down.wait_recv()

    @pl.when(has_down)
    def _():
        own_up.wait_recv()

    weights_here(2)

    def beside(at):
        conv[at] += taps_dot(2, at)

    loop(clips // chunk, beside)
    weights_here(3)

    @pl.when(s > 0)
    def _():
        for g in range(halves):

            @pl.when(has_up)
            def _():
                old_down[g].wait_recv()

            @pl.when(has_down)
            def _():
                old_up[g].wait_recv()

    for copy in small[3:]:
        copy.wait()
    conv_bias = conv_bias_ref[...].reshape(1, ch)
    attn_gain = attn_gain_ref[...].reshape(1, ch)
    triple_bias = triple_bias_ref[...].reshape(1, 3 * ch)
    output_bias = output_bias_ref[...].reshape(1, ch)

    def late(at):
        total = conv[at] + taps_dot(3, at)
        column = lax.rem(lax.broadcasted_iota(jnp.int32, (places, ch), 0), cols)
        left = pltpu.roll(total[:, :ch], 1, 0)
        right = pltpu.roll(total[:, 2 * ch :], places - 1, 0)
        summed = total[:, ch : 2 * ch] + jnp.where(column == 0, 0.0, left)
        summed = summed + jnp.where(column == cols - 1, 0.0, right)
        summed = summed + conv_bias
        at_frames = pl.ds(at * 2 * chunk, 2 * chunk)
        held = residual[at_frames].reshape(places, ch).astype(f32)
        held = (held + summed).astype(bf16)
        residual[at_frames] = held.reshape(2 * chunk, cols, ch)
        wide = held.astype(f32)
        mean = jnp.mean(wide * wide, axis=-1, keepdims=True)
        wide = (wide * lax.rsqrt(mean + EPSILON) * attn_gain).astype(bf16)
        normed[at_frames] = wide.reshape(2 * chunk, cols, ch)

    for b in range(clips):
        for t in range(2):
            residual[2 * b + t] = seg_ref[b, t, 0]
    loop(clips // chunk, late)

    there = []
    for k in range(1, n_rows):
        peer = lax.rem(r + k, n_rows)
        copy = remote(
            normed.at[pl.ds(peer * per, per)],
            gathered.at[r],
            to_send.at[k - 1],
            to_recv.at[k - 1],
            {"rows": peer},
        )
        copy.start()
        there.append(copy)
    gathered[r] = normed[pl.ds(r * per, per)]
    triple_copy.wait()
    output_copy.wait()
    for copy in there:
        copy.wait_recv()

    groups = max(1, n_rows * cols // 128)
    height = n_rows // groups

    for frame in range(per):

        def project(at):
            x = gathered[pl.ds(at * height, height), frame].reshape(height * cols, ch)
            packed = jnp.dot(x, tbuf[:, ch:], preferred_element_type=f32)
            packed = packed + triple_bias[:, ch:]
            rows = pl.ds(at * height * cols, height * cols)
            kbuf[rows] = packed[:, :ch]
            vbuf[rows] = packed[:, ch:].astype(bf16)

        def attend_rows(at):
            x = gathered[pl.ds(at * height, height), frame].reshape(height * cols, ch)
            queries = jnp.dot(x, tbuf[:, :ch], preferred_element_type=f32)
            queries = queries + triple_bias[:, :ch]
            scores = lax.dot_general(
                queries,
                kbuf[...],
                (((1,), (1,)), ((), ())),
                precision=lax.Precision.HIGHEST,
                preferred_element_type=f32,
            ) / math.sqrt(ch)
            exponent = jnp.exp(scores - jnp.max(scores, axis=-1, keepdims=True))
            weights = (exponent / jnp.sum(exponent, axis=-1, keepdims=True)).astype(bf16)
            attended = jnp.dot(weights, vbuf[...], preferred_element_type=f32).astype(bf16)
            projected = jnp.dot(attended, obuf[...], preferred_element_type=f32)
            projected = (projected + output_bias).astype(bf16)
            result[pl.ds(at * height, height), frame] = projected.reshape(height, cols, ch)

        loop(groups, project)
        loop(groups, attend_rows)

    back = []
    for k in range(1, n_rows):
        peer = lax.rem(r + k, n_rows)
        copy = remote(
            result.at[peer],
            returned.at[pl.ds(r * per, per)],
            back_send.at[k - 1],
            back_recv.at[k - 1],
            {"rows": peer},
        )
        copy.start()
        back.append(copy)
    returned[pl.ds(r * per, per)] = result[r]
    for copy in back:
        copy.wait_recv()

    for b in range(clips):
        count = len_ref[0, b]
        for t in range(2):
            f = 2 * b + t
            live = (count > t).astype(f32)
            summed = residual[f].astype(f32) + returned[f].astype(f32)
            out_ref[b, t, 0] = (summed * live).astype(bf16)

    for copy in there + back:
        copy.wait_send()

    @pl.when(s + 1 < n_tm)
    def _():
        to_flag.wait_send()
        for copy in to_next:
            copy.wait_send()

    @pl.when(s + 2 < n_tm)
    def _():
        for copy in to_after:
            copy.wait_send()

    @pl.when(has_down)
    def _():
        own_down.wait_send()

        @pl.when(s > 0)
        def _():
            for copy in old_down:
                copy.wait_send()

    @pl.when(has_up)
    def _():
        own_up.wait_send()

        @pl.when(s > 0)
        def _():
            for copy in old_up:
                copy.wait_send()


def segment(
    n_tm,
    n_rows,
    segment_input,
    inner_input,
    lengths,
    inner_gain,
    causal_weight,
    causal_bias,
    attention_gain,
    triple_weight,
    triple_bias,
    output_weight,
    output_bias,
):
    clips, _, _, cols, ch = segment_input.shape
    frames = 2 * clips
    per = frames // n_rows
    chunk = 2 - clips % 2
    bf16, f32 = jnp.bfloat16, jnp.float32
    vmem = pl.BlockSpec(memory_space=pltpu.VMEM)
    hbm = pl.BlockSpec(memory_space=pl.ANY)
    dma = pltpu.SemaphoreType.DMA
    return pl.pallas_call(
        functools.partial(segment_kernel, n_tm, n_rows, clips, cols, ch),
        out_shape=jax.ShapeDtypeStruct(segment_input.shape, bf16),
        in_specs=[hbm] * 11,
        out_specs=vmem,
        scratch_shapes=[
            pltpu.VMEM(segment_input.shape, bf16),
            pltpu.VMEM(inner_input.shape, bf16),
            pltpu.SMEM((1, clips), jnp.int32),
            pltpu.VMEM((ch,), f32),
            pltpu.VMEM((ch,), f32),
            pltpu.VMEM((ch,), f32),
            pltpu.VMEM((3 * ch,), f32),
            pltpu.VMEM((ch,), f32),
            dma((8,)),
            pltpu.VMEM((3, clips, 4, cols, ch), bf16),
            pltpu.VMEM((clips, 2, cols, ch), bf16),
            pltpu.VMEM((clips, cols, ch), bf16),
            pltpu.VMEM((clips, cols, ch), bf16),
            pltpu.VMEM((clips, 8, ch), f32),
            pltpu.VMEM((clips, 8, ch), f32),
            pltpu.VMEM((9 * ch, 3 * ch), bf16),
            pltpu.VMEM((ch, 3 * ch), bf16),
            pltpu.VMEM((ch, ch), bf16),
            pltpu.VMEM((clips // chunk, 2 * chunk * cols, 3 * ch), f32),
            pltpu.VMEM((frames, cols, ch), bf16),
            pltpu.VMEM((frames, cols, ch), bf16),
            pltpu.VMEM((n_rows, per, cols, ch), bf16),
            pltpu.VMEM((n_rows * cols, ch), f32),
            pltpu.VMEM((n_rows * cols, ch), bf16),
            pltpu.VMEM((n_rows, per, cols, ch), bf16),
            pltpu.VMEM((frames, cols, ch), bf16),
            dma((9,)),
            dma((2,)),
            dma((6,)),
            dma((6,)),
            dma((5,)),
            dma((5,)),
            dma((n_rows - 1,)),
            dma((n_rows - 1,)),
            dma((n_rows - 1,)),
            dma((n_rows - 1,)),
        ],
        compiler_params=pltpu.CompilerParams(
            collective_id=0, has_side_effects=True, vmem_limit_bytes=56 * 1024 * 1024
        ),
        name="segment",
    )(
        segment_input,
        inner_input,
        lengths.T,
        inner_gain,
        causal_weight,
        causal_bias,
        attention_gain,
        triple_weight,
        triple_bias,
        output_weight,
        output_bias,
    )


def solution(mesh):
    placed = (
        P("clips", "tm", "rows", None, None),
        P("clips", "tm", "rows", None, None),
        P("clips", "tm"),
        P(),
        P(),
        P(),
        P(),
        P(),
        P(),
        P(),
        P(),
    )
    return jax.shard_map(
        functools.partial(segment, mesh.shape["tm"], mesh.shape["rows"]),
        mesh=mesh,
        in_specs=placed,
        out_specs=P("clips", "tm", "rows", None, None),
        check_vma=False,
    )
```

```python
import functools
import math

import jax
import jax.numpy as jnp
from jax import lax
from jax.experimental import pallas as pl
from jax.experimental.pallas import tpu as pltpu
from jax.sharding import PartitionSpec as P

EPSILON = 1e-06


def loop(count, step):
    if count == 1:
        step(0)
    else:

        def one(index, carry):
            step(index)
            return carry

        lax.fori_loop(0, count, one, 0)


TAPS = ((2, 1), (1, 1), (0, 1), (2, 0), (2, 2), (1, 0), (1, 2), (0, 0), (0, 2))
STAGES = ((0, 1), (1, 3), (3, 5), (5, 9))


def segment_kernel(
    n_tm,
    n_rows,
    clips,
    cols,
    ch,
    seg_any,
    inner_any,
    len_any,
    inner_gain_any,
    weight_ref,
    conv_bias_any,
    attn_gain_any,
    triple_ref,
    triple_bias_any,
    output_ref,
    output_bias_any,
    out_ref,
    seg_ref,
    inner_ref,
    len_ref,
    inner_gain_ref,
    conv_bias_ref,
    attn_gain_ref,
    triple_bias_ref,
    output_bias_ref,
    insem,
    ext,
    prev,
    prev2,
    last,
    flag_out,
    flag_in,
    wbuf,
    tbuf,
    obuf,
    conv,
    residual,
    normed,
    gathered,
    kbuf,
    vbuf,
    result,
    returned,
    wsem,
    psem,
    near_send,
    near_recv,
    tm_send,
    tm_recv,
    to_send,
    to_recv,
    back_send,
    back_recv,
):
    s = lax.axis_index("tm")
    r = lax.axis_index("rows")
    frames = 2 * clips
    per = frames // n_rows
    chunk = 2 - clips % 2
    places = 2 * chunk * cols
    halves = 2 if clips % 2 == 0 else 1
    share = clips // halves
    bf16, f32 = jnp.bfloat16, jnp.float32

    barrier = pltpu.get_barrier_semaphore()
    for k in range(1, n_rows):
        pl.semaphore_signal(
            barrier,
            inc=1,
            device_id={"rows": lax.rem(r + k, n_rows)},
            device_id_type=pl.DeviceIdType.MESH,
        )
    expected = n_rows - 1
    for k in (-2, -1, 1, 2):
        there = jnp.logical_and(s + k >= 0, s + k < n_tm)
        expected = expected + there.astype(jnp.int32)

        @pl.when(there)
        def _():
            pl.semaphore_signal(
                barrier, inc=1, device_id={"tm": s + k}, device_id_type=pl.DeviceIdType.MESH
            )

    small = [
        pltpu.make_async_copy(src, dst, insem.at[i])
        for i, (src, dst) in enumerate(
            (
                (inner_any, inner_ref),
                (inner_gain_any, inner_gain_ref),
                (len_any, len_ref),
                (seg_any, seg_ref),
                (conv_bias_any, conv_bias_ref),
                (attn_gain_any, attn_gain_ref),
                (triple_bias_any, triple_bias_ref),
                (output_bias_any, output_bias_ref),
            )
        )
    ]
    for copy in small:
        copy.start()

    weight_copies = [
        pltpu.make_async_copy(weight_ref.at[kt, kh], wbuf.at[i], wsem.at[i])
        for i, (kt, kh) in enumerate(TAPS)
    ]
    triple_copy = pltpu.make_async_copy(triple_ref, tbuf, psem.at[0])
    output_copy = pltpu.make_async_copy(output_ref, obuf, psem.at[1])
    for copy in weight_copies[:3]:
        copy.start()

    for copy in small[:3]:
        copy.wait()
    inner_gain = inner_gain_ref[...].reshape(1, ch)

    for b in range(clips):
        for t in range(2):
            field = inner_ref[b, t, 0].astype(f32)
            mean = jnp.mean(field * field, axis=-1, keepdims=True)
            v = field * lax.rsqrt(mean + EPSILON) * inner_gain
            ext[1, b, 2 + t] = (v / (1.0 + jnp.exp(-v))).astype(bf16)
        count = len_ref[0, b]
        both = count == 2
        first = ext[1, b, 2].astype(f32)
        second = ext[1, b, 3].astype(f32)
        last[b] = jnp.where(both, second, first).astype(bf16)
        flag_out[b] = jnp.full((8, ch), count.astype(f32), f32)

    own, cached = pl.ds(2, 2), pl.ds(0, 2)
    blank = jnp.zeros((clips, 2, cols, ch), bf16)

    @pl.when(r == 0)
    def _():
        ext[0] = jnp.zeros((clips, 4, cols, ch), bf16)

    @pl.when(r == n_rows - 1)
    def _():
        ext[2] = jnp.zeros((clips, 4, cols, ch), bf16)

    @pl.when(s == 0)
    def _():
        ext[1, :, cached] = blank
        prev[...] = blank
        flag_in[...] = jnp.zeros((clips, 8, ch), f32)

        @pl.when(r > 0)
        def _():
            ext[0, :, cached] = blank

        @pl.when(r < n_rows - 1)
        def _():
            ext[2, :, cached] = blank

    @pl.when(s <= 1)
    def _():
        prev2[...] = jnp.zeros((clips, cols, ch), bf16)

    def remote(src, dst, send, recv, where):
        return pltpu.make_async_remote_copy(
            src_ref=src,
            dst_ref=dst,
            send_sem=send,
            recv_sem=recv,
            device_id=where,
            device_id_type=pl.DeviceIdType.MESH,
        )

    down, up = {"rows": r + 1}, {"rows": r - 1}
    has_down, has_up = r < n_rows - 1, r > 0
    own_down = remote(ext.at[1, :, own], ext.at[0, :, own], near_send.at[0], near_recv.at[0], down)
    own_up = remote(ext.at[1, :, own], ext.at[2, :, own], near_send.at[1], near_recv.at[1], up)
    to_flag = remote(flag_out, flag_in, tm_send.at[0], tm_recv.at[0], {"tm": s + 1})
    old_down, old_up, to_next, to_after = [], [], [], []
    for g in range(halves):
        part = pl.ds(g * share, share)
        mine = ext.at[1, part, cached]
        i, j = 2 + 2 * g, 3 + 2 * g
        old_down.append(
            remote(mine, ext.at[0, part, cached], near_send.at[i], near_recv.at[i], down)
        )
        old_up.append(remote(mine, ext.at[2, part, cached], near_send.at[j], near_recv.at[j], up))
        i, j = 1 + 2 * g, 2 + 2 * g
        to_next.append(
            remote(
                ext.at[1, part, own], prev.at[part], tm_send.at[i], tm_recv.at[i], {"tm": s + 1}
            )
        )
        to_after.append(
            remote(last.at[part], prev2.at[part], tm_send.at[j], tm_recv.at[j], {"tm": s + 2})
        )

    pl.semaphore_wait(barrier, expected)

    @pl.when(s + 1 < n_tm)
    def _():
        to_flag.start()

    for g in range(halves):

        @pl.when(s + 1 < n_tm)
        def _():
            to_next[g].start()

        @pl.when(s + 2 < n_tm)
        def _():
            to_after[g].start()

    @pl.when(has_down)
    def _():
        own_down.start()

    @pl.when(has_up)
    def _():
        own_up.start()

    for copy in weight_copies[3:]:
        copy.start()
    triple_copy.start()
    output_copy.start()

    def taps_dot(stage, at):
        begin, end = STAGES[stage]
        parts = [
            ext[kh, pl.ds(at * chunk, chunk), kt : kt + 2].reshape(places, ch)
            for kt, kh in TAPS[begin:end]
        ]
        columns = [
            jnp.concatenate([wbuf[i, kw] for i in range(begin, end)], axis=0) for kw in range(3)
        ]
        return jnp.dot(
            jnp.concatenate(parts, axis=-1),
            jnp.concatenate(columns, axis=-1),
            preferred_element_type=f32,
        )

    def weights_here(stage):
        for i in range(*STAGES[stage]):
            weight_copies[i].wait()

    def start(at):
        conv[at] = taps_dot(0, at)

    weights_here(0)
    loop(clips // chunk, start)

    @pl.when(s > 0)
    def _():
        to_flag.wait_recv()
        for g in range(halves):
            to_next[g].wait_recv()

            @pl.when(s > 1)
            def _():
                to_after[g].wait_recv()

            for b in range(g * share, (g + 1) * share):
                both = flag_in[b, 0:1, :] > 1.5
                first = prev[b, 0].astype(f32)
                second = prev[b, 1].astype(f32)
                older = prev2[b].astype(f32)
                ext[1, b, 1] = jnp.where(both, second, first).astype(bf16)
                ext[1, b, 0] = jnp.where(both, first, older).astype(bf16)

            @pl.when(has_down)
            def _():
                old_down[g].start()

            @pl.when(has_up)
            def _():
                old_up[g].start()

    weights_here(1)

    def center(at):
        conv[at] += taps_dot(1, at)

    loop(clips // chunk, center)

    @pl.when(has_up)
    def _():
        own_down.wait_recv()

    @pl.when(has_down)
    def _():
        own_up.wait_recv()

    weights_here(2)

    def beside(at):
        conv[at] += taps_dot(2, at)

    loop(clips // chunk, beside)
    weights_here(3)

    @pl.when(s > 0)
    def _():
        for g in range(halves):

            @pl.when(has_up)
            def _():
                old_down[g].wait_recv()

            @pl.when(has_down)
            def _():
                old_up[g].wait_recv()

    for copy in small[3:]:
        copy.wait()
    conv_bias = conv_bias_ref[...].reshape(1, ch)
    attn_gain = attn_gain_ref[...].reshape(1, ch)
    triple_bias = triple_bias_ref[...].reshape(1, 3 * ch)
    output_bias = output_bias_ref[...].reshape(1, ch)

    def late(at):
        total = conv[at] + taps_dot(3, at)
        column = lax.rem(lax.broadcasted_iota(jnp.int32, (places, ch), 0), cols)
        left = pltpu.roll(total[:, :ch], 1, 0)
        right = pltpu.roll(total[:, 2 * ch :], places - 1, 0)
        summed = total[:, ch : 2 * ch] + jnp.where(column == 0, 0.0, left)
        summed = summed + jnp.where(column == cols - 1, 0.0, right)
        summed = summed + conv_bias
        at_frames = pl.ds(at * 2 * chunk, 2 * chunk)
        held = residual[at_frames].reshape(places, ch).astype(f32)
        held = (held + summed).astype(bf16)
        residual[at_frames] = held.reshape(2 * chunk, cols, ch)
        wide = held.astype(f32)
        mean = jnp.mean(wide * wide, axis=-1, keepdims=True)
        wide = (wide * lax.rsqrt(mean + EPSILON) * attn_gain).astype(bf16)
        normed[at_frames] = wide.reshape(2 * chunk, cols, ch)

    for b in range(clips):
        for t in range(2):
            residual[2 * b + t] = seg_ref[b, t, 0]
    loop(clips // chunk, late)

    there = []
    for k in range(1, n_rows):
        peer = lax.rem(r + k, n_rows)
        copy = remote(
            normed.at[pl.ds(peer * per, per)],
            gathered.at[r],
            to_send.at[k - 1],
            to_recv.at[k - 1],
            {"rows": peer},
        )
        copy.start()
        there.append(copy)
    gathered[r] = normed[pl.ds(r * per, per)]
    triple_copy.wait()
    output_copy.wait()
    for copy in there:
        copy.wait_recv()

    groups = max(1, n_rows * cols // 128)
    height = n_rows // groups

    for frame in range(per):

        def project(at):
            x = gathered[pl.ds(at * height, height), frame].reshape(height * cols, ch)
            packed = jnp.dot(x, tbuf[:, ch:], preferred_element_type=f32)
            packed = packed + triple_bias[:, ch:]
            rows = pl.ds(at * height * cols, height * cols)
            kbuf[rows] = packed[:, :ch]
            vbuf[rows] = packed[:, ch:].astype(bf16)

        def attend_rows(at):
            x = gathered[pl.ds(at * height, height), frame].reshape(height * cols, ch)
            queries = jnp.dot(x, tbuf[:, :ch], preferred_element_type=f32)
            queries = queries + triple_bias[:, :ch]
            scores = lax.dot_general(
                queries,
                kbuf[...],
                (((1,), (1,)), ((), ())),
                precision=lax.Precision.HIGHEST,
                preferred_element_type=f32,
            ) / math.sqrt(ch)
            exponent = jnp.exp(scores - jnp.max(scores, axis=-1, keepdims=True))
            weights = (exponent / jnp.sum(exponent, axis=-1, keepdims=True)).astype(bf16)
            attended = jnp.dot(weights, vbuf[...], preferred_element_type=f32).astype(bf16)
            projected = jnp.dot(attended, obuf[...], preferred_element_type=f32)
            projected = (projected + output_bias).astype(bf16)
            result[pl.ds(at * height, height), frame] = projected.reshape(height, cols, ch)

        loop(groups, project)
        loop(groups, attend_rows)

    back = []
    for k in range(1, n_rows):
        peer = lax.rem(r + k, n_rows)
        copy = remote(
            result.at[peer],
            returned.at[pl.ds(r * per, per)],
            back_send.at[k - 1],
            back_recv.at[k - 1],
            {"rows": peer},
        )
        copy.start()
        back.append(copy)
    returned[pl.ds(r * per, per)] = result[r]
    for copy in back:
        copy.wait_recv()

    for b in range(clips):
        count = len_ref[0, b]
        for t in range(2):
            f = 2 * b + t
            live = (count > t).astype(f32)
            summed = residual[f].astype(f32) + returned[f].astype(f32)
            out_ref[b, t, 0] = (summed * live).astype(bf16)

    for copy in there + back:
        copy.wait_send()

    @pl.when(s + 1 < n_tm)
    def _():
        to_flag.wait_send()
        for copy in to_next:
            copy.wait_send()

    @pl.when(s + 2 < n_tm)
    def _():
        for copy in to_after:
            copy.wait_send()

    @pl.when(has_down)
    def _():
        own_down.wait_send()

        @pl.when(s > 0)
        def _():
            for copy in old_down:
                copy.wait_send()

    @pl.when(has_up)
    def _():
        own_up.wait_send()

        @pl.when(s > 0)
        def _():
            for copy in old_up:
                copy.wait_send()


def segment(
    n_tm,
    n_rows,
    segment_input,
    inner_input,
    lengths,
    inner_gain,
    causal_weight,
    causal_bias,
    attention_gain,
    triple_weight,
    triple_bias,
    output_weight,
    output_bias,
):
    clips, _, _, cols, ch = segment_input.shape
    frames = 2 * clips
    per = frames // n_rows
    chunk = 2 - clips % 2
    bf16, f32 = jnp.bfloat16, jnp.float32
    vmem = pl.BlockSpec(memory_space=pltpu.VMEM)
    hbm = pl.BlockSpec(memory_space=pl.ANY)
    dma = pltpu.SemaphoreType.DMA
    return pl.pallas_call(
        functools.partial(segment_kernel, n_tm, n_rows, clips, cols, ch),
        out_shape=jax.ShapeDtypeStruct(segment_input.shape, bf16),
        in_specs=[hbm] * 11,
        out_specs=vmem,
        scratch_shapes=[
            pltpu.VMEM(segment_input.shape, bf16),
            pltpu.VMEM(inner_input.shape, bf16),
            pltpu.SMEM((1, clips), jnp.int32),
            pltpu.VMEM((ch,), f32),
            pltpu.VMEM((ch,), f32),
            pltpu.VMEM((ch,), f32),
            pltpu.VMEM((3 * ch,), f32),
            pltpu.VMEM((ch,), f32),
            dma((8,)),
            pltpu.VMEM((3, clips, 4, cols, ch), bf16),
            pltpu.VMEM((clips, 2, cols, ch), bf16),
            pltpu.VMEM((clips, cols, ch), bf16),
            pltpu.VMEM((clips, cols, ch), bf16),
            pltpu.VMEM((clips, 8, ch), f32),
            pltpu.VMEM((clips, 8, ch), f32),
            pltpu.VMEM((9, 3, ch, ch), bf16),
            pltpu.VMEM((ch, 3 * ch), bf16),
            pltpu.VMEM((ch, ch), bf16),
            pltpu.VMEM((clips // chunk, 2 * chunk * cols, 3 * ch), f32),
            pltpu.VMEM((frames, cols, ch), bf16),
            pltpu.VMEM((frames, cols, ch), bf16),
            pltpu.VMEM((n_rows, per, cols, ch), bf16),
            pltpu.VMEM((n_rows * cols, ch), f32),
            pltpu.VMEM((n_rows * cols, ch), bf16),
            pltpu.VMEM((n_rows, per, cols, ch), bf16),
            pltpu.VMEM((frames, cols, ch), bf16),
            dma((9,)),
            dma((2,)),
            dma((6,)),
            dma((6,)),
            dma((5,)),
            dma((5,)),
            dma((n_rows - 1,)),
            dma((n_rows - 1,)),
            dma((n_rows - 1,)),
            dma((n_rows - 1,)),
        ],
        compiler_params=pltpu.CompilerParams(
            collective_id=0, has_side_effects=True, vmem_limit_bytes=56 * 1024 * 1024
        ),
        name="segment",
    )(
        segment_input,
        inner_input,
        lengths.T,
        inner_gain,
        causal_weight,
        causal_bias,
        attention_gain,
        triple_weight,
        triple_bias,
        output_weight,
        output_bias,
    )


def solution(mesh):
    placed = (
        P("clips", "tm", "rows", None, None),
        P("clips", "tm", "rows", None, None),
        P("clips", "tm"),
        P(),
        P(),
        P(),
        P(),
        P(),
        P(),
        P(),
        P(),
    )
    return jax.shard_map(
        functools.partial(segment, mesh.shape["tm"], mesh.shape["rows"]),
        mesh=mesh,
        in_specs=placed,
        out_specs=P("clips", "tm", "rows", None, None),
        check_vma=False,
    )
```

```python
import functools
import math

import jax
import jax.numpy as jnp
from jax import lax
from jax.experimental import pallas as pl
from jax.experimental.pallas import tpu as pltpu
from jax.sharding import PartitionSpec as P

EPSILON = 1e-06


def loop(count, step):
    if count == 1:
        step(0)
    else:

        def one(index, carry):
            step(index)
            return carry

        lax.fori_loop(0, count, one, 0)


TAPS = ((2, 1), (1, 1), (0, 1), (2, 0), (2, 2), (1, 0), (1, 2), (0, 0), (0, 2))
STAGES = ((0, 1), (1, 3), (3, 5), (5, 9))


def segment_kernel(
    n_tm,
    n_rows,
    clips,
    cols,
    ch,
    seg_any,
    inner_any,
    len_any,
    inner_gain_any,
    weight_ref,
    conv_bias_any,
    attn_gain_any,
    triple_ref,
    triple_bias_any,
    output_ref,
    output_bias_any,
    out_ref,
    seg_ref,
    inner_ref,
    len_ref,
    inner_gain_ref,
    conv_bias_ref,
    attn_gain_ref,
    triple_bias_ref,
    output_bias_ref,
    insem,
    ext,
    prev,
    prev2,
    last,
    flag_out,
    flag_in,
    wbuf,
    tbuf,
    obuf,
    conv,
    residual,
    normed,
    gathered,
    kbuf,
    vbuf,
    result,
    returned,
    wsem,
    psem,
    near_send,
    near_recv,
    tm_send,
    tm_recv,
    to_send,
    to_recv,
    back_send,
    back_recv,
):
    s = lax.axis_index("tm")
    r = lax.axis_index("rows")
    frames = 2 * clips
    per = frames // n_rows
    chunk = 2 - clips % 2
    halves = 2 if clips % 2 == 0 and n_rows % 2 == 0 else 1
    share = clips // halves
    step = 2 - share % 2
    bf16, f32 = jnp.bfloat16, jnp.float32

    barrier = pltpu.get_barrier_semaphore()
    for k in range(1, n_rows):
        pl.semaphore_signal(
            barrier,
            inc=1,
            device_id={"rows": lax.rem(r + k, n_rows)},
            device_id_type=pl.DeviceIdType.MESH,
        )
    expected = n_rows - 1
    for k in (-2, -1, 1, 2):
        there = jnp.logical_and(s + k >= 0, s + k < n_tm)
        expected = expected + there.astype(jnp.int32)

        @pl.when(there)
        def _():
            pl.semaphore_signal(
                barrier, inc=1, device_id={"tm": s + k}, device_id_type=pl.DeviceIdType.MESH
            )

    small = [
        pltpu.make_async_copy(src, dst, insem.at[i])
        for i, (src, dst) in enumerate(
            (
                (inner_any, inner_ref),
                (inner_gain_any, inner_gain_ref),
                (len_any, len_ref),
                (seg_any, seg_ref),
                (conv_bias_any, conv_bias_ref),
                (attn_gain_any, attn_gain_ref),
                (triple_bias_any, triple_bias_ref),
                (output_bias_any, output_bias_ref),
            )
        )
    ]
    for copy in small:
        copy.start()

    weight_copies = [
        pltpu.make_async_copy(weight_ref.at[kt, kh], wbuf.at[i], wsem.at[i])
        for i, (kt, kh) in enumerate(TAPS)
    ]
    triple_copy = pltpu.make_async_copy(triple_ref, tbuf, psem.at[0])
    output_copy = pltpu.make_async_copy(output_ref, obuf, psem.at[1])
    for copy in weight_copies[:3]:
        copy.start()

    for copy in small[:3]:
        copy.wait()
    inner_gain = inner_gain_ref[...].reshape(1, ch)

    for b in range(clips):
        for t in range(2):
            field = inner_ref[b, t, 0].astype(f32)
            mean = jnp.mean(field * field, axis=-1, keepdims=True)
            v = field * lax.rsqrt(mean + EPSILON) * inner_gain
            ext[1, b, 2 + t] = (v / (1.0 + jnp.exp(-v))).astype(bf16)
        count = len_ref[0, b]
        both = count == 2
        first = ext[1, b, 2].astype(f32)
        second = ext[1, b, 3].astype(f32)
        last[b] = jnp.where(both, second, first).astype(bf16)
        flag_out[b] = jnp.full((8, ch), count.astype(f32), f32)

    own, cached = pl.ds(2, 2), pl.ds(0, 2)
    blank = jnp.zeros((clips, 2, cols, ch), bf16)

    @pl.when(r == 0)
    def _():
        ext[0] = jnp.zeros((clips, 4, cols, ch), bf16)

    @pl.when(r == n_rows - 1)
    def _():
        ext[2] = jnp.zeros((clips, 4, cols, ch), bf16)

    @pl.when(s == 0)
    def _():
        ext[1, :, cached] = blank
        prev[...] = blank
        flag_in[...] = jnp.zeros((clips, 8, ch), f32)

        @pl.when(r > 0)
        def _():
            ext[0, :, cached] = blank

        @pl.when(r < n_rows - 1)
        def _():
            ext[2, :, cached] = blank

    @pl.when(s <= 1)
    def _():
        prev2[...] = jnp.zeros((clips, cols, ch), bf16)

    def remote(src, dst, send, recv, where):
        return pltpu.make_async_remote_copy(
            src_ref=src,
            dst_ref=dst,
            send_sem=send,
            recv_sem=recv,
            device_id=where,
            device_id_type=pl.DeviceIdType.MESH,
        )

    down, up = {"rows": r + 1}, {"rows": r - 1}
    has_down, has_up = r < n_rows - 1, r > 0
    own_down = remote(ext.at[1, :, own], ext.at[0, :, own], near_send.at[0], near_recv.at[0], down)
    own_up = remote(ext.at[1, :, own], ext.at[2, :, own], near_send.at[1], near_recv.at[1], up)
    to_flag = remote(flag_out, flag_in, tm_send.at[0], tm_recv.at[0], {"tm": s + 1})
    old_down, old_up, to_next, to_after = [], [], [], []
    for g in range(halves):
        part = pl.ds(g * share, share)
        mine = ext.at[1, part, cached]
        i, j = 2 + 2 * g, 3 + 2 * g
        old_down.append(
            remote(mine, ext.at[0, part, cached], near_send.at[i], near_recv.at[i], down)
        )
        old_up.append(remote(mine, ext.at[2, part, cached], near_send.at[j], near_recv.at[j], up))
        i, j = 1 + 2 * g, 2 + 2 * g
        to_next.append(
            remote(
                ext.at[1, part, own], prev.at[part], tm_send.at[i], tm_recv.at[i], {"tm": s + 1}
            )
        )
        to_after.append(
            remote(last.at[part], prev2.at[part], tm_send.at[j], tm_recv.at[j], {"tm": s + 2})
        )

    pl.semaphore_wait(barrier, expected)

    @pl.when(s + 1 < n_tm)
    def _():
        to_flag.start()

    for g in range(halves):

        @pl.when(s + 1 < n_tm)
        def _():
            to_next[g].start()

        @pl.when(s + 2 < n_tm)
        def _():
            to_after[g].start()

    @pl.when(has_down)
    def _():
        own_down.start()

    @pl.when(has_up)
    def _():
        own_up.start()

    for copy in weight_copies[3:]:
        copy.start()
    triple_copy.start()
    output_copy.start()

    def taps_dot(stage, at, chunk):
        begin, end = STAGES[stage]
        parts = [
            ext[kh, pl.ds(at * chunk, chunk), kt : kt + 2].reshape(2 * chunk * cols, ch)
            for kt, kh in TAPS[begin:end]
        ]
        columns = [
            jnp.concatenate([wbuf[i, kw] for i in range(begin, end)], axis=0) for kw in range(3)
        ]
        return jnp.dot(
            jnp.concatenate(parts, axis=-1),
            jnp.concatenate(columns, axis=-1),
            preferred_element_type=f32,
        )

    def weights_here(stage):
        for i in range(*STAGES[stage]):
            weight_copies[i].wait()

    def start(at):
        held = taps_dot(0, at, chunk).reshape(chunk, 2 * cols, 3 * ch)
        conv[pl.ds(at * chunk, chunk)] = held

    weights_here(0)
    loop(clips // chunk, start)

    @pl.when(s > 0)
    def _():
        to_flag.wait_recv()
        for g in range(halves):
            to_next[g].wait_recv()

            @pl.when(s > 1)
            def _():
                to_after[g].wait_recv()

            for b in range(g * share, (g + 1) * share):
                both = flag_in[b, 0:1, :] > 1.5
                first = prev[b, 0].astype(f32)
                second = prev[b, 1].astype(f32)
                older = prev2[b].astype(f32)
                ext[1, b, 1] = jnp.where(both, second, first).astype(bf16)
                ext[1, b, 0] = jnp.where(both, first, older).astype(bf16)

            @pl.when(has_down)
            def _():
                old_down[g].start()

            @pl.when(has_up)
            def _():
                old_up[g].start()

    weights_here(1)

    def center(at):
        held = taps_dot(1, at, chunk).reshape(chunk, 2 * cols, 3 * ch)
        conv[pl.ds(at * chunk, chunk)] += held

    loop(clips // chunk, center)

    @pl.when(has_up)
    def _():
        own_down.wait_recv()

    @pl.when(has_down)
    def _():
        own_up.wait_recv()

    weights_here(2)

    def beside(at):
        held = taps_dot(2, at, chunk).reshape(chunk, 2 * cols, 3 * ch)
        conv[pl.ds(at * chunk, chunk)] += held

    loop(clips // chunk, beside)
    weights_here(3)

    for copy in small[3:]:
        copy.wait()
    conv_bias = conv_bias_ref[...].reshape(1, ch)
    attn_gain = attn_gain_ref[...].reshape(1, ch)
    triple_bias = triple_bias_ref[...].reshape(1, 3 * ch)
    output_bias = output_bias_ref[...].reshape(1, ch)

    def late(at):
        places = 2 * step * cols
        total = conv[pl.ds(at * step, step)].reshape(places, 3 * ch) + taps_dot(3, at, step)
        column = lax.rem(lax.broadcasted_iota(jnp.int32, (places, ch), 0), cols)
        left = pltpu.roll(total[:, :ch], 1, 0)
        right = pltpu.roll(total[:, 2 * ch :], places - 1, 0)
        summed = total[:, ch : 2 * ch] + jnp.where(column == 0, 0.0, left)
        summed = summed + jnp.where(column == cols - 1, 0.0, right)
        summed = summed + conv_bias
        at_frames = pl.ds(at * 2 * step, 2 * step)
        held = residual[at_frames].reshape(places, ch).astype(f32)
        held = (held + summed).astype(bf16)
        residual[at_frames] = held.reshape(2 * step, cols, ch)
        wide = held.astype(f32)
        mean = jnp.mean(wide * wide, axis=-1, keepdims=True)
        wide = (wide * lax.rsqrt(mean + EPSILON) * attn_gain).astype(bf16)
        normed[at_frames] = wide.reshape(2 * step, cols, ch)

    for b in range(clips):
        for t in range(2):
            residual[2 * b + t] = seg_ref[b, t, 0]
    there = []
    for k in range(1, n_rows):
        peer = lax.rem(r + k, n_rows)
        there.append(
            remote(
                normed.at[pl.ds(peer * per, per)],
                gathered.at[r],
                to_send.at[k - 1],
                to_recv.at[k - 1],
                {"rows": peer},
            )
        )
    for g in range(halves):

        @pl.when(s > 0)
        def _():
            @pl.when(has_up)
            def _():
                old_down[g].wait_recv()

            @pl.when(has_down)
            def _():
                old_up[g].wait_recv()

        first = g * share // step
        loop(share // step, lambda at: late(first + at))
        for k in range(1, n_rows):

            @pl.when(lax.rem(r + k, n_rows) // (n_rows // halves) == g)
            def _():
                there[k - 1].start()

    gathered[r] = normed[pl.ds(r * per, per)]
    triple_copy.wait()
    output_copy.wait()
    for copy in there:
        copy.wait_recv()

    groups = max(1, n_rows * cols // 128)
    height = n_rows // groups

    for frame in range(per):

        def project(at):
            x = gathered[pl.ds(at * height, height), frame].reshape(height * cols, ch)
            packed = jnp.dot(x, tbuf[:, ch:], preferred_element_type=f32)
            packed = packed + triple_bias[:, ch:]
            rows = pl.ds(at * height * cols, height * cols)
            kbuf[rows] = packed[:, :ch]
            vbuf[rows] = packed[:, ch:].astype(bf16)

        def attend_rows(at):
            x = gathered[pl.ds(at * height, height), frame].reshape(height * cols, ch)
            queries = jnp.dot(x, tbuf[:, :ch], preferred_element_type=f32)
            queries = queries + triple_bias[:, :ch]
            scores = lax.dot_general(
                queries,
                kbuf[...],
                (((1,), (1,)), ((), ())),
                precision=lax.Precision.HIGHEST,
                preferred_element_type=f32,
            ) / math.sqrt(ch)
            exponent = jnp.exp(scores - jnp.max(scores, axis=-1, keepdims=True))
            weights = (exponent / jnp.sum(exponent, axis=-1, keepdims=True)).astype(bf16)
            attended = jnp.dot(weights, vbuf[...], preferred_element_type=f32).astype(bf16)
            projected = jnp.dot(attended, obuf[...], preferred_element_type=f32)
            projected = (projected + output_bias).astype(bf16)
            result[pl.ds(at * height, height), frame] = projected.reshape(height, cols, ch)

        loop(groups, project)
        loop(groups, attend_rows)

    back = []
    for k in range(1, n_rows):
        peer = lax.rem(r + k, n_rows)
        copy = remote(
            result.at[peer],
            returned.at[pl.ds(r * per, per)],
            back_send.at[k - 1],
            back_recv.at[k - 1],
            {"rows": peer},
        )
        copy.start()
        back.append(copy)
    returned[pl.ds(r * per, per)] = result[r]
    for copy in back:
        copy.wait_recv()

    for b in range(clips):
        count = len_ref[0, b]
        for t in range(2):
            f = 2 * b + t
            live = (count > t).astype(f32)
            summed = residual[f].astype(f32) + returned[f].astype(f32)
            out_ref[b, t, 0] = (summed * live).astype(bf16)

    for copy in there + back:
        copy.wait_send()

    @pl.when(s + 1 < n_tm)
    def _():
        to_flag.wait_send()
        for copy in to_next:
            copy.wait_send()

    @pl.when(s + 2 < n_tm)
    def _():
        for copy in to_after:
            copy.wait_send()

    @pl.when(has_down)
    def _():
        own_down.wait_send()

        @pl.when(s > 0)
        def _():
            for copy in old_down:
                copy.wait_send()

    @pl.when(has_up)
    def _():
        own_up.wait_send()

        @pl.when(s > 0)
        def _():
            for copy in old_up:
                copy.wait_send()


def segment(
    n_tm,
    n_rows,
    segment_input,
    inner_input,
    lengths,
    inner_gain,
    causal_weight,
    causal_bias,
    attention_gain,
    triple_weight,
    triple_bias,
    output_weight,
    output_bias,
):
    clips, _, _, cols, ch = segment_input.shape
    frames = 2 * clips
    per = frames // n_rows
    bf16, f32 = jnp.bfloat16, jnp.float32
    vmem = pl.BlockSpec(memory_space=pltpu.VMEM)
    hbm = pl.BlockSpec(memory_space=pl.ANY)
    dma = pltpu.SemaphoreType.DMA
    return pl.pallas_call(
        functools.partial(segment_kernel, n_tm, n_rows, clips, cols, ch),
        out_shape=jax.ShapeDtypeStruct(segment_input.shape, bf16),
        in_specs=[hbm] * 11,
        out_specs=vmem,
        scratch_shapes=[
            pltpu.VMEM(segment_input.shape, bf16),
            pltpu.VMEM(inner_input.shape, bf16),
            pltpu.SMEM((1, clips), jnp.int32),
            pltpu.VMEM((ch,), f32),
            pltpu.VMEM((ch,), f32),
            pltpu.VMEM((ch,), f32),
            pltpu.VMEM((3 * ch,), f32),
            pltpu.VMEM((ch,), f32),
            dma((8,)),
            pltpu.VMEM((3, clips, 4, cols, ch), bf16),
            pltpu.VMEM((clips, 2, cols, ch), bf16),
            pltpu.VMEM((clips, cols, ch), bf16),
            pltpu.VMEM((clips, cols, ch), bf16),
            pltpu.VMEM((clips, 8, ch), f32),
            pltpu.VMEM((clips, 8, ch), f32),
            pltpu.VMEM((9, 3, ch, ch), bf16),
            pltpu.VMEM((ch, 3 * ch), bf16),
            pltpu.VMEM((ch, ch), bf16),
            pltpu.VMEM((clips, 2 * cols, 3 * ch), f32),
            pltpu.VMEM((frames, cols, ch), bf16),
            pltpu.VMEM((frames, cols, ch), bf16),
            pltpu.VMEM((n_rows, per, cols, ch), bf16),
            pltpu.VMEM((n_rows * cols, ch), f32),
            pltpu.VMEM((n_rows * cols, ch), bf16),
            pltpu.VMEM((n_rows, per, cols, ch), bf16),
            pltpu.VMEM((frames, cols, ch), bf16),
            dma((9,)),
            dma((2,)),
            dma((6,)),
            dma((6,)),
            dma((5,)),
            dma((5,)),
            dma((n_rows - 1,)),
            dma((n_rows - 1,)),
            dma((n_rows - 1,)),
            dma((n_rows - 1,)),
        ],
        compiler_params=pltpu.CompilerParams(
            collective_id=0, has_side_effects=True, vmem_limit_bytes=56 * 1024 * 1024
        ),
        name="segment",
    )(
        segment_input,
        inner_input,
        lengths.T,
        inner_gain,
        causal_weight,
        causal_bias,
        attention_gain,
        triple_weight,
        triple_bias,
        output_weight,
        output_bias,
    )


def solution(mesh):
    placed = (
        P("clips", "tm", "rows", None, None),
        P("clips", "tm", "rows", None, None),
        P("clips", "tm"),
        P(),
        P(),
        P(),
        P(),
        P(),
        P(),
        P(),
        P(),
    )
    return jax.shard_map(
        functools.partial(segment, mesh.shape["tm"], mesh.shape["rows"]),
        mesh=mesh,
        in_specs=placed,
        out_specs=P("clips", "tm", "rows", None, None),
        check_vma=False,
    )
```

```python
import functools
import math

import jax
import jax.numpy as jnp
from jax import lax
from jax.experimental import pallas as pl
from jax.experimental.pallas import tpu as pltpu
from jax.sharding import PartitionSpec as P

EPSILON = 1e-06


def loop(count, step):
    if count == 1:
        step(0)
    else:

        def one(index, carry):
            step(index)
            return carry

        lax.fori_loop(0, count, one, 0)


TAPS = ((2, 1), (1, 1), (0, 1), (2, 0), (2, 2), (1, 0), (1, 2), (0, 0), (0, 2))
STAGES = ((0, 1), (1, 3), (3, 5), (5, 7), (7, 9))


def segment_kernel(
    n_tm,
    n_rows,
    clips,
    cols,
    ch,
    seg_any,
    inner_any,
    len_any,
    inner_gain_any,
    weight_ref,
    conv_bias_any,
    attn_gain_any,
    triple_ref,
    triple_bias_any,
    output_ref,
    output_bias_any,
    out_ref,
    seg_ref,
    inner_ref,
    len_ref,
    inner_gain_ref,
    conv_bias_ref,
    attn_gain_ref,
    triple_bias_ref,
    output_bias_ref,
    insem,
    ext,
    prev,
    prev2,
    last,
    flag_out,
    flag_in,
    wbuf,
    tbuf,
    obuf,
    conv,
    residual,
    normed,
    gathered,
    kbuf,
    vbuf,
    result,
    returned,
    wsem,
    psem,
    near_send,
    near_recv,
    tm_send,
    tm_recv,
    to_send,
    to_recv,
    back_send,
    back_recv,
):
    s = lax.axis_index("tm")
    r = lax.axis_index("rows")
    frames = 2 * clips
    per = frames // n_rows
    chunk = 2 - clips % 2
    halves = 2 if clips % 2 == 0 and n_rows % 2 == 0 else 1
    share = clips // halves
    step = 2 - share % 2
    bf16, f32 = jnp.bfloat16, jnp.float32

    barrier = pltpu.get_barrier_semaphore()
    for k in range(1, n_rows):
        pl.semaphore_signal(
            barrier,
            inc=1,
            device_id={"rows": lax.rem(r + k, n_rows)},
            device_id_type=pl.DeviceIdType.MESH,
        )
    expected = n_rows - 1
    for k in (-2, -1, 1, 2):
        there = jnp.logical_and(s + k >= 0, s + k < n_tm)
        expected = expected + there.astype(jnp.int32)

        @pl.when(there)
        def _():
            pl.semaphore_signal(
                barrier, inc=1, device_id={"tm": s + k}, device_id_type=pl.DeviceIdType.MESH
            )

    small = [
        pltpu.make_async_copy(src, dst, insem.at[i])
        for i, (src, dst) in enumerate(
            (
                (inner_any, inner_ref),
                (inner_gain_any, inner_gain_ref),
                (len_any, len_ref),
                (seg_any, seg_ref),
                (conv_bias_any, conv_bias_ref),
                (attn_gain_any, attn_gain_ref),
                (triple_bias_any, triple_bias_ref),
                (output_bias_any, output_bias_ref),
            )
        )
    ]
    for copy in small:
        copy.start()

    weight_copies = [
        pltpu.make_async_copy(weight_ref.at[kt, kh], wbuf.at[i], wsem.at[i])
        for i, (kt, kh) in enumerate(TAPS)
    ]
    triple_copy = pltpu.make_async_copy(triple_ref, tbuf, psem.at[0])
    output_copy = pltpu.make_async_copy(output_ref, obuf, psem.at[1])
    for copy in weight_copies[:3]:
        copy.start()

    for copy in small[:3]:
        copy.wait()
    inner_gain = inner_gain_ref[...].reshape(1, ch)

    for b in range(clips):
        for t in range(2):
            field = inner_ref[b, t, 0].astype(f32)
            mean = jnp.mean(field * field, axis=-1, keepdims=True)
            v = field * lax.rsqrt(mean + EPSILON) * inner_gain
            ext[1, b, 2 + t] = (v / (1.0 + jnp.exp(-v))).astype(bf16)
        count = len_ref[0, b]
        both = count == 2
        first = ext[1, b, 2].astype(f32)
        second = ext[1, b, 3].astype(f32)
        last[b] = jnp.where(both, second, first).astype(bf16)
        flag_out[b] = jnp.full((8, ch), count.astype(f32), f32)

    own, cached = pl.ds(2, 2), pl.ds(0, 2)
    blank = jnp.zeros((clips, 2, cols, ch), bf16)

    @pl.when(r == 0)
    def _():
        ext[0] = jnp.zeros((clips, 4, cols, ch), bf16)

    @pl.when(r == n_rows - 1)
    def _():
        ext[2] = jnp.zeros((clips, 4, cols, ch), bf16)

    @pl.when(s == 0)
    def _():
        ext[1, :, cached] = blank
        prev[...] = jnp.zeros((clips, cols, ch), bf16)
        flag_in[...] = jnp.zeros((clips, 8, ch), f32)

        @pl.when(r > 0)
        def _():
            ext[0, :, cached] = blank

        @pl.when(r < n_rows - 1)
        def _():
            ext[2, :, cached] = blank

    @pl.when(s <= 1)
    def _():
        prev2[...] = jnp.zeros((clips, cols, ch), bf16)

    def remote(src, dst, send, recv, where):
        return pltpu.make_async_remote_copy(
            src_ref=src,
            dst_ref=dst,
            send_sem=send,
            recv_sem=recv,
            device_id=where,
            device_id_type=pl.DeviceIdType.MESH,
        )

    down, up = {"rows": r + 1}, {"rows": r - 1}
    has_down, has_up = r < n_rows - 1, r > 0
    own_down = remote(ext.at[1, :, own], ext.at[0, :, own], near_send.at[0], near_recv.at[0], down)
    own_up = remote(ext.at[1, :, own], ext.at[2, :, own], near_send.at[1], near_recv.at[1], up)
    old_down, old_up = [], []
    for slot in range(2):
        mine = ext.at[1, :, slot]
        i, j = 2 + 2 * slot, 3 + 2 * slot
        old_down.append(remote(mine, ext.at[0, :, slot], near_send.at[i], near_recv.at[i], down))
        old_up.append(remote(mine, ext.at[2, :, slot], near_send.at[j], near_recv.at[j], up))
    after, later = {"tm": s + 1}, {"tm": s + 2}
    to_flag = remote(flag_out, flag_in, tm_send.at[0], tm_recv.at[0], after)
    to_last = remote(last, ext.at[1, :, 1], tm_send.at[1], tm_recv.at[1], after)
    to_first = remote(ext.at[1, :, 2], prev, tm_send.at[2], tm_recv.at[2], after)
    to_after = remote(last, prev2, tm_send.at[3], tm_recv.at[3], later)

    pl.semaphore_wait(barrier, expected)

    @pl.when(s + 1 < n_tm)
    def _():
        to_last.start()
        to_flag.start()
        to_first.start()

    @pl.when(s + 2 < n_tm)
    def _():
        to_after.start()

    @pl.when(has_down)
    def _():
        own_down.start()

    @pl.when(has_up)
    def _():
        own_up.start()

    for copy in weight_copies[3:]:
        copy.start()
    triple_copy.start()
    output_copy.start()

    def taps_dot(stage, at, chunk):
        begin, end = STAGES[stage]
        parts = [
            ext[kh, pl.ds(at * chunk, chunk), kt : kt + 2].reshape(2 * chunk * cols, ch)
            for kt, kh in TAPS[begin:end]
        ]
        columns = [
            jnp.concatenate([wbuf[i, kw] for i in range(begin, end)], axis=0) for kw in range(3)
        ]
        return jnp.dot(
            jnp.concatenate(parts, axis=-1),
            jnp.concatenate(columns, axis=-1),
            preferred_element_type=f32,
        )

    def weights_here(stage):
        for i in range(*STAGES[stage]):
            weight_copies[i].wait()

    def start(at):
        held = taps_dot(0, at, chunk).reshape(chunk, 2 * cols, 3 * ch)
        conv[pl.ds(at * chunk, chunk)] = held

    weights_here(0)
    loop(clips // chunk, start)

    def pass_on(slot):
        @pl.when(has_down)
        def _():
            old_down[slot].start()

        @pl.when(has_up)
        def _():
            old_up[slot].start()

    def passed_on(slot):
        @pl.when(s > 0)
        def _():
            @pl.when(has_up)
            def _():
                old_down[slot].wait_recv()

            @pl.when(has_down)
            def _():
                old_up[slot].wait_recv()

    @pl.when(s > 0)
    def _():
        to_last.wait_recv()
        pass_on(1)
        to_flag.wait_recv()
        to_first.wait_recv()

        @pl.when(s > 1)
        def _():
            to_after.wait_recv()

        for b in range(clips):
            both = flag_in[b, 0:1, :] > 1.5
            older = jnp.where(both, prev[b].astype(f32), prev2[b].astype(f32))
            ext[1, b, 0] = older.astype(bf16)
        pass_on(0)

    weights_here(1)

    def center(at):
        held = taps_dot(1, at, chunk).reshape(chunk, 2 * cols, 3 * ch)
        conv[pl.ds(at * chunk, chunk)] += held

    loop(clips // chunk, center)

    @pl.when(has_up)
    def _():
        own_down.wait_recv()

    @pl.when(has_down)
    def _():
        own_up.wait_recv()

    weights_here(2)

    def beside(at):
        held = taps_dot(2, at, chunk).reshape(chunk, 2 * cols, 3 * ch)
        conv[pl.ds(at * chunk, chunk)] += held

    loop(clips // chunk, beside)
    weights_here(3)
    passed_on(1)

    def nearer(at):
        held = taps_dot(3, at, chunk).reshape(chunk, 2 * cols, 3 * ch)
        conv[pl.ds(at * chunk, chunk)] += held

    loop(clips // chunk, nearer)
    weights_here(4)
    passed_on(0)

    for copy in small[3:]:
        copy.wait()
    conv_bias = conv_bias_ref[...].reshape(1, ch)
    attn_gain = attn_gain_ref[...].reshape(1, ch)
    triple_bias = triple_bias_ref[...].reshape(1, 3 * ch)
    output_bias = output_bias_ref[...].reshape(1, ch)

    def late(at):
        places = 2 * step * cols
        total = conv[pl.ds(at * step, step)].reshape(places, 3 * ch) + taps_dot(4, at, step)
        column = lax.rem(lax.broadcasted_iota(jnp.int32, (places, ch), 0), cols)
        left = pltpu.roll(total[:, :ch], 1, 0)
        right = pltpu.roll(total[:, 2 * ch :], places - 1, 0)
        summed = total[:, ch : 2 * ch] + jnp.where(column == 0, 0.0, left)
        summed = summed + jnp.where(column == cols - 1, 0.0, right)
        summed = summed + conv_bias
        at_frames = pl.ds(at * 2 * step, 2 * step)
        held = residual[at_frames].reshape(places, ch).astype(f32)
        held = (held + summed).astype(bf16)
        residual[at_frames] = held.reshape(2 * step, cols, ch)
        wide = held.astype(f32)
        mean = jnp.mean(wide * wide, axis=-1, keepdims=True)
        wide = (wide * lax.rsqrt(mean + EPSILON) * attn_gain).astype(bf16)
        normed[at_frames] = wide.reshape(2 * step, cols, ch)

    for b in range(clips):
        for t in range(2):
            residual[2 * b + t] = seg_ref[b, t, 0]
    there = []
    for k in range(1, n_rows):
        peer = lax.rem(r + k, n_rows)
        there.append(
            remote(
                normed.at[pl.ds(peer * per, per)],
                gathered.at[r],
                to_send.at[k - 1],
                to_recv.at[k - 1],
                {"rows": peer},
            )
        )
    for g in range(halves):
        first = g * share // step
        loop(share // step, lambda at: late(first + at))
        for k in range(1, n_rows):

            @pl.when(lax.rem(r + k, n_rows) // (n_rows // halves) == g)
            def _():
                there[k - 1].start()

    gathered[r] = normed[pl.ds(r * per, per)]
    triple_copy.wait()
    output_copy.wait()
    for copy in there:
        copy.wait_recv()

    groups = max(1, n_rows * cols // 128)
    height = n_rows // groups

    for frame in range(per):

        def project(at):
            x = gathered[pl.ds(at * height, height), frame].reshape(height * cols, ch)
            packed = jnp.dot(x, tbuf[:, ch:], preferred_element_type=f32)
            packed = packed + triple_bias[:, ch:]
            rows = pl.ds(at * height * cols, height * cols)
            kbuf[rows] = packed[:, :ch]
            vbuf[rows] = packed[:, ch:].astype(bf16)

        def attend_rows(at):
            x = gathered[pl.ds(at * height, height), frame].reshape(height * cols, ch)
            queries = jnp.dot(x, tbuf[:, :ch], preferred_element_type=f32)
            queries = queries + triple_bias[:, :ch]
            scores = lax.dot_general(
                queries,
                kbuf[...],
                (((1,), (1,)), ((), ())),
                precision=lax.Precision.HIGHEST,
                preferred_element_type=f32,
            ) / math.sqrt(ch)
            exponent = jnp.exp(scores - jnp.max(scores, axis=-1, keepdims=True))
            weights = (exponent / jnp.sum(exponent, axis=-1, keepdims=True)).astype(bf16)
            attended = jnp.dot(weights, vbuf[...], preferred_element_type=f32).astype(bf16)
            projected = jnp.dot(attended, obuf[...], preferred_element_type=f32)
            projected = (projected + output_bias).astype(bf16)
            result[pl.ds(at * height, height), frame] = projected.reshape(height, cols, ch)

        loop(groups, project)
        loop(groups, attend_rows)

    back = []
    for k in range(1, n_rows):
        peer = lax.rem(r + k, n_rows)
        copy = remote(
            result.at[peer],
            returned.at[pl.ds(r * per, per)],
            back_send.at[k - 1],
            back_recv.at[k - 1],
            {"rows": peer},
        )
        copy.start()
        back.append(copy)
    returned[pl.ds(r * per, per)] = result[r]
    for copy in back:
        copy.wait_recv()

    for b in range(clips):
        count = len_ref[0, b]
        for t in range(2):
            f = 2 * b + t
            live = (count > t).astype(f32)
            summed = residual[f].astype(f32) + returned[f].astype(f32)
            out_ref[b, t, 0] = (summed * live).astype(bf16)

    for copy in there + back:
        copy.wait_send()

    @pl.when(s + 1 < n_tm)
    def _():
        to_flag.wait_send()
        to_last.wait_send()
        to_first.wait_send()

    @pl.when(s + 2 < n_tm)
    def _():
        to_after.wait_send()

    @pl.when(has_down)
    def _():
        own_down.wait_send()

        @pl.when(s > 0)
        def _():
            for copy in old_down:
                copy.wait_send()

    @pl.when(has_up)
    def _():
        own_up.wait_send()

        @pl.when(s > 0)
        def _():
            for copy in old_up:
                copy.wait_send()


def segment(
    n_tm,
    n_rows,
    segment_input,
    inner_input,
    lengths,
    inner_gain,
    causal_weight,
    causal_bias,
    attention_gain,
    triple_weight,
    triple_bias,
    output_weight,
    output_bias,
):
    clips, _, _, cols, ch = segment_input.shape
    frames = 2 * clips
    per = frames // n_rows
    bf16, f32 = jnp.bfloat16, jnp.float32
    vmem = pl.BlockSpec(memory_space=pltpu.VMEM)
    hbm = pl.BlockSpec(memory_space=pl.ANY)
    dma = pltpu.SemaphoreType.DMA
    return pl.pallas_call(
        functools.partial(segment_kernel, n_tm, n_rows, clips, cols, ch),
        out_shape=jax.ShapeDtypeStruct(segment_input.shape, bf16),
        in_specs=[hbm] * 11,
        out_specs=vmem,
        scratch_shapes=[
            pltpu.VMEM(segment_input.shape, bf16),
            pltpu.VMEM(inner_input.shape, bf16),
            pltpu.SMEM((1, clips), jnp.int32),
            pltpu.VMEM((ch,), f32),
            pltpu.VMEM((ch,), f32),
            pltpu.VMEM((ch,), f32),
            pltpu.VMEM((3 * ch,), f32),
            pltpu.VMEM((ch,), f32),
            dma((8,)),
            pltpu.VMEM((3, clips, 4, cols, ch), bf16),
            pltpu.VMEM((clips, cols, ch), bf16),
            pltpu.VMEM((clips, cols, ch), bf16),
            pltpu.VMEM((clips, cols, ch), bf16),
            pltpu.VMEM((clips, 8, ch), f32),
            pltpu.VMEM((clips, 8, ch), f32),
            pltpu.VMEM((9, 3, ch, ch), bf16),
            pltpu.VMEM((ch, 3 * ch), bf16),
            pltpu.VMEM((ch, ch), bf16),
            pltpu.VMEM((clips, 2 * cols, 3 * ch), f32),
            pltpu.VMEM((frames, cols, ch), bf16),
            pltpu.VMEM((frames, cols, ch), bf16),
            pltpu.VMEM((n_rows, per, cols, ch), bf16),
            pltpu.VMEM((n_rows * cols, ch), f32),
            pltpu.VMEM((n_rows * cols, ch), bf16),
            pltpu.VMEM((n_rows, per, cols, ch), bf16),
            pltpu.VMEM((frames, cols, ch), bf16),
            dma((9,)),
            dma((2,)),
            dma((6,)),
            dma((6,)),
            dma((4,)),
            dma((4,)),
            dma((n_rows - 1,)),
            dma((n_rows - 1,)),
            dma((n_rows - 1,)),
            dma((n_rows - 1,)),
        ],
        compiler_params=pltpu.CompilerParams(
            collective_id=0, has_side_effects=True, vmem_limit_bytes=56 * 1024 * 1024
        ),
        name="segment",
    )(
        segment_input,
        inner_input,
        lengths.T,
        inner_gain,
        causal_weight,
        causal_bias,
        attention_gain,
        triple_weight,
        triple_bias,
        output_weight,
        output_bias,
    )


def solution(mesh):
    placed = (
        P("clips", "tm", "rows", None, None),
        P("clips", "tm", "rows", None, None),
        P("clips", "tm"),
        P(),
        P(),
        P(),
        P(),
        P(),
        P(),
        P(),
        P(),
    )
    return jax.shard_map(
        functools.partial(segment, mesh.shape["tm"], mesh.shape["rows"]),
        mesh=mesh,
        in_specs=placed,
        out_specs=P("clips", "tm", "rows", None, None),
        check_vma=False,
    )
```

```python
import functools
import math

import jax
import jax.numpy as jnp
from jax import lax
from jax.experimental import pallas as pl
from jax.experimental.pallas import tpu as pltpu
from jax.sharding import PartitionSpec as P

EPSILON = 1e-06


def loop(count, step):
    if count == 1:
        step(0)
    else:

        def one(index, carry):
            step(index)
            return carry

        lax.fori_loop(0, count, one, 0)


TAPS = ((2, 1), (1, 1), (0, 1), (2, 0), (2, 2), (1, 0), (1, 2), (0, 0), (0, 2))
STAGES = ((0, 1), (1, 3), (3, 5), (5, 7), (7, 9))


def segment_kernel(
    n_tm,
    n_rows,
    clips,
    cols,
    ch,
    seg_any,
    inner_any,
    len_any,
    inner_gain_any,
    weight_ref,
    conv_bias_any,
    attn_gain_any,
    triple_ref,
    triple_bias_any,
    output_ref,
    output_bias_any,
    out_ref,
    seg_ref,
    inner_ref,
    len_ref,
    inner_gain_ref,
    conv_bias_ref,
    attn_gain_ref,
    triple_bias_ref,
    output_bias_ref,
    insem,
    ext,
    prev,
    prev2,
    last,
    flag_out,
    flag_in,
    wbuf,
    tbuf,
    obuf,
    conv,
    residual,
    normed,
    gathered,
    qbuf,
    kbuf,
    vbuf,
    result,
    returned,
    wsem,
    psem,
    near_send,
    near_recv,
    tm_send,
    tm_recv,
    to_send,
    to_recv,
    back_send,
    back_recv,
):
    s = lax.axis_index("tm")
    r = lax.axis_index("rows")
    frames = 2 * clips
    per = frames // n_rows
    chunk = 2 - clips % 2
    halves = 2 if clips % 2 == 0 and n_rows % 2 == 0 else 1
    share = clips // halves
    step = 2 - share % 2
    bf16, f32 = jnp.bfloat16, jnp.float32

    barrier = pltpu.get_barrier_semaphore()
    for k in range(1, n_rows):
        pl.semaphore_signal(
            barrier,
            inc=1,
            device_id={"rows": lax.rem(r + k, n_rows)},
            device_id_type=pl.DeviceIdType.MESH,
        )
    expected = n_rows - 1
    for k in (-2, -1, 1, 2):
        there = jnp.logical_and(s + k >= 0, s + k < n_tm)
        expected = expected + there.astype(jnp.int32)

        @pl.when(there)
        def _():
            pl.semaphore_signal(
                barrier, inc=1, device_id={"tm": s + k}, device_id_type=pl.DeviceIdType.MESH
            )

    small = [
        pltpu.make_async_copy(src, dst, insem.at[i])
        for i, (src, dst) in enumerate(
            (
                (inner_any, inner_ref),
                (inner_gain_any, inner_gain_ref),
                (len_any, len_ref),
                (seg_any, seg_ref),
                (conv_bias_any, conv_bias_ref),
                (attn_gain_any, attn_gain_ref),
                (triple_bias_any, triple_bias_ref),
                (output_bias_any, output_bias_ref),
            )
        )
    ]
    for copy in small:
        copy.start()

    weight_copies = [
        pltpu.make_async_copy(weight_ref.at[kt, kh], wbuf.at[i], wsem.at[i])
        for i, (kt, kh) in enumerate(TAPS)
    ]
    triple_copy = pltpu.make_async_copy(triple_ref, tbuf, psem.at[0])
    output_copy = pltpu.make_async_copy(output_ref, obuf, psem.at[1])
    for copy in weight_copies + [triple_copy, output_copy]:
        copy.start(priority=1)

    for copy in small[:3]:
        copy.wait()
    inner_gain = inner_gain_ref[...].reshape(1, ch)

    for b in range(clips):
        for t in range(2):
            field = inner_ref[b, t, 0].astype(f32)
            mean = jnp.mean(field * field, axis=-1, keepdims=True)
            v = field * lax.rsqrt(mean + EPSILON) * inner_gain
            ext[1, b, 2 + t] = (v / (1.0 + jnp.exp(-v))).astype(bf16)
        count = len_ref[0, b]
        both = count == 2
        first = ext[1, b, 2].astype(f32)
        second = ext[1, b, 3].astype(f32)
        last[b] = jnp.where(both, second, first).astype(bf16)
        flag_out[b] = jnp.full((8, ch), count.astype(f32), f32)

    own, cached = pl.ds(2, 2), pl.ds(0, 2)
    blank = jnp.zeros((clips, 2, cols, ch), bf16)

    @pl.when(r == 0)
    def _():
        ext[0] = jnp.zeros((clips, 4, cols, ch), bf16)

    @pl.when(r == n_rows - 1)
    def _():
        ext[2] = jnp.zeros((clips, 4, cols, ch), bf16)

    @pl.when(s == 0)
    def _():
        ext[1, :, cached] = blank
        prev[...] = jnp.zeros((clips, cols, ch), bf16)
        flag_in[...] = jnp.zeros((clips, 8, ch), f32)

        @pl.when(r > 0)
        def _():
            ext[0, :, cached] = blank

        @pl.when(r < n_rows - 1)
        def _():
            ext[2, :, cached] = blank

    @pl.when(s <= 1)
    def _():
        prev2[...] = jnp.zeros((clips, cols, ch), bf16)

    def remote(src, dst, send, recv, where):
        return pltpu.make_async_remote_copy(
            src_ref=src,
            dst_ref=dst,
            send_sem=send,
            recv_sem=recv,
            device_id=where,
            device_id_type=pl.DeviceIdType.MESH,
        )

    down, up = {"rows": r + 1}, {"rows": r - 1}
    has_down, has_up = r < n_rows - 1, r > 0
    own_down = remote(ext.at[1, :, own], ext.at[0, :, own], near_send.at[0], near_recv.at[0], down)
    own_up = remote(ext.at[1, :, own], ext.at[2, :, own], near_send.at[1], near_recv.at[1], up)
    old_down, old_up = [], []
    for slot in range(2):
        mine = ext.at[1, :, slot]
        i, j = 2 + 2 * slot, 3 + 2 * slot
        old_down.append(remote(mine, ext.at[0, :, slot], near_send.at[i], near_recv.at[i], down))
        old_up.append(remote(mine, ext.at[2, :, slot], near_send.at[j], near_recv.at[j], up))
    after, later = {"tm": s + 1}, {"tm": s + 2}
    to_flag = remote(flag_out, flag_in, tm_send.at[0], tm_recv.at[0], after)
    to_last = remote(last, ext.at[1, :, 1], tm_send.at[1], tm_recv.at[1], after)
    to_first = remote(ext.at[1, :, 2], prev, tm_send.at[2], tm_recv.at[2], after)
    to_after = remote(last, prev2, tm_send.at[3], tm_recv.at[3], later)

    pl.semaphore_wait(barrier, expected)

    @pl.when(s + 1 < n_tm)
    def _():
        to_last.start()
        to_flag.start()
        to_first.start()

    @pl.when(s + 2 < n_tm)
    def _():
        to_after.start()

    @pl.when(has_down)
    def _():
        own_down.start()

    @pl.when(has_up)
    def _():
        own_up.start()


    def taps_dot(stage, at, chunk):
        begin, end = STAGES[stage]
        parts = [
            ext[kh, pl.ds(at * chunk, chunk), kt : kt + 2].reshape(2 * chunk * cols, ch)
            for kt, kh in TAPS[begin:end]
        ]
        columns = [
            jnp.concatenate([wbuf[i, kw] for i in range(begin, end)], axis=0) for kw in range(3)
        ]
        return jnp.dot(
            jnp.concatenate(parts, axis=-1),
            jnp.concatenate(columns, axis=-1),
            preferred_element_type=f32,
        )

    def weights_here(stage):
        for i in range(*STAGES[stage]):
            weight_copies[i].wait()

    def start(at):
        held = taps_dot(0, at, chunk).reshape(chunk, 2 * cols, 3 * ch)
        conv[pl.ds(at * chunk, chunk)] = held

    weights_here(0)
    loop(clips // chunk, start)

    def pass_on(slot):
        @pl.when(has_down)
        def _():
            old_down[slot].start()

        @pl.when(has_up)
        def _():
            old_up[slot].start()

    def passed_on(slot):
        @pl.when(s > 0)
        def _():
            @pl.when(has_up)
            def _():
                old_down[slot].wait_recv()

            @pl.when(has_down)
            def _():
                old_up[slot].wait_recv()

    @pl.when(s > 0)
    def _():
        to_last.wait_recv()
        pass_on(1)
        to_flag.wait_recv()
        to_first.wait_recv()

        @pl.when(s > 1)
        def _():
            to_after.wait_recv()

        for b in range(clips):
            both = flag_in[b, 0:1, :] > 1.5
            older = jnp.where(both, prev[b].astype(f32), prev2[b].astype(f32))
            ext[1, b, 0] = older.astype(bf16)
        pass_on(0)

    weights_here(1)

    def center(at):
        held = taps_dot(1, at, chunk).reshape(chunk, 2 * cols, 3 * ch)
        conv[pl.ds(at * chunk, chunk)] += held

    loop(clips // chunk, center)

    @pl.when(has_up)
    def _():
        own_down.wait_recv()

    @pl.when(has_down)
    def _():
        own_up.wait_recv()

    weights_here(2)

    def beside(at):
        held = taps_dot(2, at, chunk).reshape(chunk, 2 * cols, 3 * ch)
        conv[pl.ds(at * chunk, chunk)] += held

    loop(clips // chunk, beside)
    weights_here(3)
    passed_on(1)

    def nearer(at):
        held = taps_dot(3, at, chunk).reshape(chunk, 2 * cols, 3 * ch)
        conv[pl.ds(at * chunk, chunk)] += held

    loop(clips // chunk, nearer)
    weights_here(4)
    passed_on(0)

    for copy in small[3:]:
        copy.wait()
    conv_bias = conv_bias_ref[...].reshape(1, ch)
    attn_gain = attn_gain_ref[...].reshape(1, ch)
    triple_bias = triple_bias_ref[...].reshape(1, 3 * ch)
    output_bias = output_bias_ref[...].reshape(1, ch)

    def late(at):
        places = 2 * step * cols
        total = conv[pl.ds(at * step, step)].reshape(places, 3 * ch) + taps_dot(4, at, step)
        column = lax.rem(lax.broadcasted_iota(jnp.int32, (places, ch), 0), cols)
        left = pltpu.roll(total[:, :ch], 1, 0)
        right = pltpu.roll(total[:, 2 * ch :], places - 1, 0)
        summed = total[:, ch : 2 * ch] + jnp.where(column == 0, 0.0, left)
        summed = summed + jnp.where(column == cols - 1, 0.0, right)
        summed = summed + conv_bias
        at_frames = pl.ds(at * 2 * step, 2 * step)
        held = residual[at_frames].reshape(places, ch).astype(f32)
        held = (held + summed).astype(bf16)
        residual[at_frames] = held.reshape(2 * step, cols, ch)
        wide = held.astype(f32)
        mean = jnp.mean(wide * wide, axis=-1, keepdims=True)
        wide = (wide * lax.rsqrt(mean + EPSILON) * attn_gain).astype(bf16)
        normed[at_frames] = wide.reshape(2 * step, cols, ch)

    for b in range(clips):
        for t in range(2):
            residual[2 * b + t] = seg_ref[b, t, 0]
    there = []
    for k in range(1, n_rows):
        peer = lax.rem(r + k, n_rows)
        there.append(
            remote(
                normed.at[pl.ds(peer * per, per)],
                gathered.at[r],
                to_send.at[k - 1],
                to_recv.at[k - 1],
                {"rows": peer},
            )
        )
    for g in range(halves):
        first = g * share // step
        loop(share // step, lambda at: late(first + at))
        for k in range(1, n_rows):

            @pl.when(lax.rem(r + k, n_rows) // (n_rows // halves) == g)
            def _():
                there[k - 1].start()

    gathered[r] = normed[pl.ds(r * per, per)]
    triple_copy.wait()
    output_copy.wait()
    for copy in there:
        copy.wait_recv()

    block = n_rows if n_rows % 4 else 4
    group = n_rows if n_rows % 2 else 2 if n_rows == 4 else block
    turns = n_rows // group
    back = []
    for k in range(1, n_rows):
        peer = lax.rem(r + k, n_rows)
        back.append(
            remote(
                result.at[peer],
                returned.at[pl.ds(r * per, per)],
                back_send.at[k - 1],
                back_recv.at[k - 1],
                {"rows": peer},
            )
        )

    for frame in range(per):

        def project(at):
            x = gathered[pl.ds(at * block, block), frame].reshape(block * cols, ch)
            packed = jnp.dot(x, tbuf[...], preferred_element_type=f32) + triple_bias
            rows = pl.ds(at * block * cols, block * cols)
            qbuf[rows] = packed[:, :ch]
            kbuf[rows] = packed[:, ch : 2 * ch]
            vbuf[rows] = packed[:, 2 * ch :].astype(bf16)

        def attend_rows(turn):
            at = lax.rem(r // group + turns // 2 + turn, turns)
            queries = qbuf[pl.ds(at * group * cols, group * cols)]
            scores = lax.dot_general(
                queries,
                kbuf[...],
                (((1,), (1,)), ((), ())),
                precision=lax.Precision.HIGHEST,
                preferred_element_type=f32,
            ) / math.sqrt(ch)
            exponent = jnp.exp(scores - jnp.max(scores, axis=-1, keepdims=True))
            weights = (exponent / jnp.sum(exponent, axis=-1, keepdims=True)).astype(bf16)
            attended = jnp.dot(weights, vbuf[...], preferred_element_type=f32).astype(bf16)
            projected = jnp.dot(attended, obuf[...], preferred_element_type=f32)
            projected = (projected + output_bias).astype(bf16)
            result[pl.ds(at * group, group), frame] = projected.reshape(group, cols, ch)
            if frame == per - 1:
                for k in range(1, n_rows):

                    @pl.when(lax.rem(r + k, n_rows) // group == at)
                    def _():
                        back[k - 1].start()

        loop(n_rows // block, project)
        if turns <= 2:
            for turn in range(turns):
                attend_rows(turn)
        else:
            loop(turns, attend_rows)

    returned[pl.ds(r * per, per)] = result[r]
    for copy in back:
        copy.wait_recv()

    for b in range(clips):
        count = len_ref[0, b]
        for t in range(2):
            f = 2 * b + t
            live = (count > t).astype(f32)
            summed = residual[f].astype(f32) + returned[f].astype(f32)
            out_ref[b, t, 0] = (summed * live).astype(bf16)

    for copy in there + back:
        copy.wait_send()

    @pl.when(s + 1 < n_tm)
    def _():
        to_flag.wait_send()
        to_last.wait_send()
        to_first.wait_send()

    @pl.when(s + 2 < n_tm)
    def _():
        to_after.wait_send()

    @pl.when(has_down)
    def _():
        own_down.wait_send()

        @pl.when(s > 0)
        def _():
            for copy in old_down:
                copy.wait_send()

    @pl.when(has_up)
    def _():
        own_up.wait_send()

        @pl.when(s > 0)
        def _():
            for copy in old_up:
                copy.wait_send()


def segment(
    n_tm,
    n_rows,
    segment_input,
    inner_input,
    lengths,
    inner_gain,
    causal_weight,
    causal_bias,
    attention_gain,
    triple_weight,
    triple_bias,
    output_weight,
    output_bias,
):
    clips, _, _, cols, ch = segment_input.shape
    frames = 2 * clips
    per = frames // n_rows
    bf16, f32 = jnp.bfloat16, jnp.float32
    vmem = pl.BlockSpec(memory_space=pltpu.VMEM)
    hbm = pl.BlockSpec(memory_space=pl.ANY)
    dma = pltpu.SemaphoreType.DMA
    return pl.pallas_call(
        functools.partial(segment_kernel, n_tm, n_rows, clips, cols, ch),
        out_shape=jax.ShapeDtypeStruct(segment_input.shape, bf16),
        in_specs=[hbm] * 11,
        out_specs=vmem,
        scratch_shapes=[
            pltpu.VMEM(segment_input.shape, bf16),
            pltpu.VMEM(inner_input.shape, bf16),
            pltpu.SMEM((1, clips), jnp.int32),
            pltpu.VMEM((ch,), f32),
            pltpu.VMEM((ch,), f32),
            pltpu.VMEM((ch,), f32),
            pltpu.VMEM((3 * ch,), f32),
            pltpu.VMEM((ch,), f32),
            dma((8,)),
            pltpu.VMEM((3, clips, 4, cols, ch), bf16),
            pltpu.VMEM((clips, cols, ch), bf16),
            pltpu.VMEM((clips, cols, ch), bf16),
            pltpu.VMEM((clips, cols, ch), bf16),
            pltpu.VMEM((clips, 8, ch), f32),
            pltpu.VMEM((clips, 8, ch), f32),
            pltpu.VMEM((9, 3, ch, ch), bf16),
            pltpu.VMEM((ch, 3 * ch), bf16),
            pltpu.VMEM((ch, ch), bf16),
            pltpu.VMEM((clips, 2 * cols, 3 * ch), f32),
            pltpu.VMEM((frames, cols, ch), bf16),
            pltpu.VMEM((frames, cols, ch), bf16),
            pltpu.VMEM((n_rows, per, cols, ch), bf16),
            pltpu.VMEM((n_rows * cols, ch), f32),
            pltpu.VMEM((n_rows * cols, ch), f32),
            pltpu.VMEM((n_rows * cols, ch), bf16),
            pltpu.VMEM((n_rows, per, cols, ch), bf16),
            pltpu.VMEM((frames, cols, ch), bf16),
            dma((9,)),
            dma((2,)),
            dma((6,)),
            dma((6,)),
            dma((4,)),
            dma((4,)),
            dma((n_rows - 1,)),
            dma((n_rows - 1,)),
            dma((n_rows - 1,)),
            dma((n_rows - 1,)),
        ],
        compiler_params=pltpu.CompilerParams(
            collective_id=0, has_side_effects=True, vmem_limit_bytes=56 * 1024 * 1024
        ),
        name="segment",
    )(
        segment_input,
        inner_input,
        lengths.T,
        inner_gain,
        causal_weight,
        causal_bias,
        attention_gain,
        triple_weight,
        triple_bias,
        output_weight,
        output_bias,
    )


def solution(mesh):
    placed = (
        P("clips", "tm", "rows", None, None),
        P("clips", "tm", "rows", None, None),
        P("clips", "tm"),
        P(),
        P(),
        P(),
        P(),
        P(),
        P(),
        P(),
        P(),
    )
    return jax.shard_map(
        functools.partial(segment, mesh.shape["tm"], mesh.shape["rows"]),
        mesh=mesh,
        in_specs=placed,
        out_specs=P("clips", "tm", "rows", None, None),
        check_vma=False,
    )
```

```python
import functools
import math

import jax
import jax.numpy as jnp
from jax import lax
from jax.experimental import pallas as pl
from jax.experimental.pallas import tpu as pltpu
from jax.sharding import PartitionSpec as P

EPSILON = 1e-06


def loop(count, step):
    if count == 1:
        step(0)
    else:

        def one(index, carry):
            step(index)
            return carry

        lax.fori_loop(0, count, one, 0)


TAPS = ((2, 1), (1, 1), (0, 1), (2, 0), (2, 2), (1, 0), (1, 2), (0, 0), (0, 2))
STAGES = ((0, 1), (1, 3), (3, 5), (5, 7), (7, 9))


def segment_kernel(
    n_tm,
    n_rows,
    clips,
    cols,
    ch,
    seg_any,
    inner_any,
    len_any,
    inner_gain_any,
    weight_ref,
    conv_bias_any,
    attn_gain_any,
    triple_ref,
    triple_bias_any,
    output_ref,
    output_bias_any,
    out_ref,
    seg_ref,
    inner_ref,
    len_ref,
    inner_gain_ref,
    conv_bias_ref,
    attn_gain_ref,
    triple_bias_ref,
    output_bias_ref,
    insem,
    ext,
    prev,
    prev2,
    last,
    flag_out,
    flag_in,
    wbuf,
    tbuf,
    obuf,
    conv,
    residual,
    normed,
    gathered,
    qbuf,
    kbuf,
    vbuf,
    result,
    returned,
    wsem,
    psem,
    near_send,
    near_recv,
    tm_send,
    tm_recv,
    to_send,
    to_recv,
    back_send,
    back_recv,
):
    s = lax.axis_index("tm")
    r = lax.axis_index("rows")
    frames = 2 * clips
    per = frames // n_rows
    chunk = 2 - clips % 2
    halves = 2 if clips % 2 == 0 and n_rows % 2 == 0 else 1
    share = clips // halves
    step = 2 - share % 2
    bf16, f32 = jnp.bfloat16, jnp.float32

    barrier = pltpu.get_barrier_semaphore()
    for k in range(1, n_rows):
        pl.semaphore_signal(
            barrier,
            inc=1,
            device_id={"rows": lax.rem(r + k, n_rows)},
            device_id_type=pl.DeviceIdType.MESH,
        )
    expected = n_rows - 1
    for k in (-2, -1, 1, 2):
        there = jnp.logical_and(s + k >= 0, s + k < n_tm)
        expected = expected + there.astype(jnp.int32)

        @pl.when(there)
        def _():
            pl.semaphore_signal(
                barrier, inc=1, device_id={"tm": s + k}, device_id_type=pl.DeviceIdType.MESH
            )

    small = [
        pltpu.make_async_copy(src, dst, insem.at[i])
        for i, (src, dst) in enumerate(
            (
                (inner_any, inner_ref),
                (inner_gain_any, inner_gain_ref),
                (len_any, len_ref),
                (seg_any, seg_ref),
                (conv_bias_any, conv_bias_ref),
                (attn_gain_any, attn_gain_ref),
                (triple_bias_any, triple_bias_ref),
                (output_bias_any, output_bias_ref),
            )
        )
    ]
    for copy in small:
        copy.start()

    weight_copies = [
        pltpu.make_async_copy(weight_ref.at[kt, kh], wbuf.at[i], wsem.at[i])
        for i, (kt, kh) in enumerate(TAPS)
    ]
    triple_copy = pltpu.make_async_copy(triple_ref, tbuf, psem.at[0])
    output_copy = pltpu.make_async_copy(output_ref, obuf, psem.at[1])
    for copy in weight_copies + [triple_copy, output_copy]:
        copy.start(priority=1)

    for copy in small[:3]:
        copy.wait()
    inner_gain = inner_gain_ref[...].reshape(1, ch)

    for b in range(clips):
        for t in range(2):
            field = inner_ref[b, t, 0].astype(f32)
            mean = jnp.mean(field * field, axis=-1, keepdims=True)
            v = field * lax.rsqrt(mean + EPSILON) * inner_gain
            ext[1, b, 2 + t] = (v / (1.0 + jnp.exp(-v))).astype(bf16)
        count = len_ref[0, b]
        both = count == 2
        first = ext[1, b, 2].astype(f32)
        second = ext[1, b, 3].astype(f32)
        last[b] = jnp.where(both, second, first).astype(bf16)
        flag_out[b] = jnp.full((8, ch), count.astype(f32), f32)

    own, cached = pl.ds(2, 2), pl.ds(0, 2)
    blank = jnp.zeros((clips, 2, cols, ch), bf16)

    @pl.when(r == 0)
    def _():
        ext[0] = jnp.zeros((clips, 4, cols, ch), bf16)

    @pl.when(r == n_rows - 1)
    def _():
        ext[2] = jnp.zeros((clips, 4, cols, ch), bf16)

    @pl.when(s == 0)
    def _():
        ext[1, :, cached] = blank
        prev[...] = jnp.zeros((clips, cols, ch), bf16)
        flag_in[...] = jnp.zeros((clips, 8, ch), f32)

        @pl.when(r > 0)
        def _():
            ext[0, :, cached] = blank

        @pl.when(r < n_rows - 1)
        def _():
            ext[2, :, cached] = blank

    @pl.when(s <= 1)
    def _():
        prev2[...] = jnp.zeros((clips, cols, ch), bf16)

    def remote(src, dst, send, recv, where):
        return pltpu.make_async_remote_copy(
            src_ref=src,
            dst_ref=dst,
            send_sem=send,
            recv_sem=recv,
            device_id=where,
            device_id_type=pl.DeviceIdType.MESH,
        )

    down, up = {"rows": r + 1}, {"rows": r - 1}
    has_down, has_up = r < n_rows - 1, r > 0
    own_down = remote(ext.at[1, :, own], ext.at[0, :, own], near_send.at[0], near_recv.at[0], down)
    own_up = remote(ext.at[1, :, own], ext.at[2, :, own], near_send.at[1], near_recv.at[1], up)
    old_down, old_up = [], []
    for slot in range(2):
        mine = ext.at[1, :, slot]
        i, j = 2 + 2 * slot, 3 + 2 * slot
        old_down.append(remote(mine, ext.at[0, :, slot], near_send.at[i], near_recv.at[i], down))
        old_up.append(remote(mine, ext.at[2, :, slot], near_send.at[j], near_recv.at[j], up))
    after, later = {"tm": s + 1}, {"tm": s + 2}
    to_flag = remote(flag_out, flag_in, tm_send.at[0], tm_recv.at[0], after)
    to_last = remote(last, ext.at[1, :, 1], tm_send.at[1], tm_recv.at[1], after)
    to_first = remote(ext.at[1, :, 2], prev, tm_send.at[2], tm_recv.at[2], after)
    to_after = remote(last, prev2, tm_send.at[3], tm_recv.at[3], later)

    pl.semaphore_wait(barrier, expected)

    @pl.when(s + 1 < n_tm)
    def _():
        to_last.start()
        to_flag.start()
        to_first.start()

    @pl.when(s + 2 < n_tm)
    def _():
        to_after.start()

    @pl.when(has_down)
    def _():
        own_down.start()

    @pl.when(has_up)
    def _():
        own_up.start()


    def taps_dot(stage, at, chunk):
        begin, end = STAGES[stage]
        parts = [
            ext[kh, pl.ds(at * chunk, chunk), kt : kt + 2].reshape(2 * chunk * cols, ch)
            for kt, kh in TAPS[begin:end]
        ]
        columns = [
            jnp.concatenate([wbuf[i, kw] for i in range(begin, end)], axis=0) for kw in range(3)
        ]
        return jnp.dot(
            jnp.concatenate(parts, axis=-1),
            jnp.concatenate(columns, axis=-1),
            preferred_element_type=f32,
        )

    def weights_here(stage):
        for i in range(*STAGES[stage]):
            weight_copies[i].wait()

    def start(at):
        held = taps_dot(0, at, chunk).reshape(chunk, 2 * cols, 3 * ch)
        conv[pl.ds(at * chunk, chunk)] = held

    weights_here(0)
    loop(clips // chunk, start)

    def pass_on(slot):
        @pl.when(has_down)
        def _():
            old_down[slot].start()

        @pl.when(has_up)
        def _():
            old_up[slot].start()

    def passed_on(slot):
        @pl.when(s > 0)
        def _():
            @pl.when(has_up)
            def _():
                old_down[slot].wait_recv()

            @pl.when(has_down)
            def _():
                old_up[slot].wait_recv()

    @pl.when(s > 0)
    def _():
        to_last.wait_recv()
        pass_on(1)
        to_flag.wait_recv()
        to_first.wait_recv()

        @pl.when(s > 1)
        def _():
            to_after.wait_recv()

        for b in range(clips):
            both = flag_in[b, 0:1, :] > 1.5
            older = jnp.where(both, prev[b].astype(f32), prev2[b].astype(f32))
            ext[1, b, 0] = older.astype(bf16)
        pass_on(0)

    weights_here(1)

    def center(at):
        held = taps_dot(1, at, chunk).reshape(chunk, 2 * cols, 3 * ch)
        conv[pl.ds(at * chunk, chunk)] += held

    loop(clips // chunk, center)

    @pl.when(has_up)
    def _():
        own_down.wait_recv()

    @pl.when(has_down)
    def _():
        own_up.wait_recv()

    weights_here(2)

    def beside(at):
        held = taps_dot(2, at, chunk).reshape(chunk, 2 * cols, 3 * ch)
        conv[pl.ds(at * chunk, chunk)] += held

    loop(clips // chunk, beside)
    weights_here(3)
    passed_on(1)

    def nearer(at):
        held = taps_dot(3, at, chunk).reshape(chunk, 2 * cols, 3 * ch)
        conv[pl.ds(at * chunk, chunk)] += held

    loop(clips // chunk, nearer)
    weights_here(4)
    passed_on(0)

    for copy in small[3:]:
        copy.wait()
    conv_bias = conv_bias_ref[...].reshape(1, ch)
    attn_gain = attn_gain_ref[...].reshape(1, ch)
    triple_bias = triple_bias_ref[...].reshape(1, 3 * ch)
    output_bias = output_bias_ref[...].reshape(1, ch)

    def late(at):
        places = 2 * step * cols
        total = conv[pl.ds(at * step, step)].reshape(places, 3 * ch) + taps_dot(4, at, step)
        column = lax.rem(lax.broadcasted_iota(jnp.int32, (places, ch), 0), cols)
        left = pltpu.roll(total[:, :ch], 1, 0)
        right = pltpu.roll(total[:, 2 * ch :], places - 1, 0)
        summed = total[:, ch : 2 * ch] + jnp.where(column == 0, 0.0, left)
        summed = summed + jnp.where(column == cols - 1, 0.0, right)
        summed = summed + conv_bias
        at_frames = pl.ds(at * 2 * step, 2 * step)
        held = residual[at_frames].reshape(places, ch).astype(f32)
        held = (held + summed).astype(bf16)
        residual[at_frames] = held.reshape(2 * step, cols, ch)
        wide = held.astype(f32)
        mean = jnp.mean(wide * wide, axis=-1, keepdims=True)
        wide = (wide * lax.rsqrt(mean + EPSILON) * attn_gain).astype(bf16)
        normed[at_frames] = wide.reshape(2 * step, cols, ch)

    for b in range(clips):
        for t in range(2):
            residual[2 * b + t] = seg_ref[b, t, 0]
    there = []
    for k in range(1, n_rows):
        peer = lax.rem(r + k, n_rows)
        there.append(
            remote(
                normed.at[pl.ds(peer * per, per)],
                gathered.at[r],
                to_send.at[k - 1],
                to_recv.at[k - 1],
                {"rows": peer},
            )
        )
    for g in range(halves):
        first = g * share // step
        loop(share // step, lambda at: late(first + at))
        for k in range(1, n_rows):

            @pl.when(lax.rem(r + k, n_rows) // (n_rows // halves) == g)
            def _():
                there[k - 1].start()

    gathered[r] = normed[pl.ds(r * per, per)]
    triple_copy.wait()
    output_copy.wait()
    for copy in there:
        copy.wait_recv()

    block = n_rows if n_rows % 4 else 4
    group = n_rows if n_rows % 2 else 2 if n_rows == 4 else block
    turns = n_rows // group
    back = []
    for k in range(1, n_rows):
        peer = lax.rem(r + k, n_rows)
        back.append(
            remote(
                result.at[peer],
                returned.at[pl.ds(r * per, per)],
                back_send.at[k - 1],
                back_recv.at[k - 1],
                {"rows": peer},
            )
        )

    for frame in range(per):

        def project(at):
            x = gathered[pl.ds(at * block, block), frame].reshape(block * cols, ch)
            packed = jnp.dot(x, tbuf[...], preferred_element_type=f32) + triple_bias
            rows = pl.ds(at * block * cols, block * cols)
            qbuf[rows] = packed[:, :ch]
            kbuf[rows] = packed[:, ch : 2 * ch]
            vbuf[rows] = packed[:, 2 * ch :].astype(bf16)

        def attend_rows(turn):
            at = lax.rem(r // group + turns // 2 + turn, turns)
            queries = qbuf[pl.ds(at * group * cols, group * cols)]
            scores = lax.dot_general(
                queries,
                kbuf[...],
                (((1,), (1,)), ((), ())),
                precision=lax.Precision.HIGHEST,
                preferred_element_type=f32,
            ) / math.sqrt(ch)
            exponent = jnp.exp(scores - jnp.max(scores, axis=-1, keepdims=True))
            weights = (exponent / jnp.sum(exponent, axis=-1, keepdims=True)).astype(bf16)
            attended = jnp.dot(weights, vbuf[...], preferred_element_type=f32).astype(bf16)
            projected = jnp.dot(attended, obuf[...], preferred_element_type=f32)
            projected = (projected + output_bias).astype(bf16)
            result[pl.ds(at * group, group), frame] = projected.reshape(group, cols, ch)
            if frame == per - 1:
                for k in range(1, n_rows):

                    @pl.when(lax.rem(r + k, n_rows) // group == at)
                    def _():
                        back[k - 1].start()

        loop(n_rows // block, project)
        if turns <= 2:
            for turn in range(turns):
                attend_rows(turn)
        else:
            loop(turns, attend_rows)

    returned[pl.ds(r * per, per)] = result[r]
    for copy in back:
        copy.wait_recv()

    for b in range(clips):
        count = len_ref[0, b]
        for t in range(2):
            f = 2 * b + t
            live = (count > t).astype(f32)
            summed = residual[f].astype(f32) + returned[f].astype(f32)
            out_ref[b, t, 0] = (summed * live).astype(bf16)

    for copy in there + back:
        copy.wait_send()

    @pl.when(s + 1 < n_tm)
    def _():
        to_flag.wait_send()
        to_last.wait_send()
        to_first.wait_send()

    @pl.when(s + 2 < n_tm)
    def _():
        to_after.wait_send()

    @pl.when(has_down)
    def _():
        own_down.wait_send()

        @pl.when(s > 0)
        def _():
            for copy in old_down:
                copy.wait_send()

    @pl.when(has_up)
    def _():
        own_up.wait_send()

        @pl.when(s > 0)
        def _():
            for copy in old_up:
                copy.wait_send()


def segment(
    n_tm,
    n_rows,
    segment_input,
    inner_input,
    lengths,
    inner_gain,
    causal_weight,
    causal_bias,
    attention_gain,
    triple_weight,
    triple_bias,
    output_weight,
    output_bias,
):
    clips, _, _, cols, ch = segment_input.shape
    frames = 2 * clips
    per = frames // n_rows
    bf16, f32 = jnp.bfloat16, jnp.float32
    vmem = pl.BlockSpec(memory_space=pltpu.VMEM)
    hbm = pl.BlockSpec(memory_space=pl.ANY)
    dma = pltpu.SemaphoreType.DMA
    return pl.pallas_call(
        functools.partial(segment_kernel, n_tm, n_rows, clips, cols, ch),
        out_shape=pltpu.VMEM(segment_input.shape, bf16),
        in_specs=[hbm] * 11,
        out_specs=vmem,
        scratch_shapes=[
            pltpu.VMEM(segment_input.shape, bf16),
            pltpu.VMEM(inner_input.shape, bf16),
            pltpu.SMEM((1, clips), jnp.int32),
            pltpu.VMEM((ch,), f32),
            pltpu.VMEM((ch,), f32),
            pltpu.VMEM((ch,), f32),
            pltpu.VMEM((3 * ch,), f32),
            pltpu.VMEM((ch,), f32),
            dma((8,)),
            pltpu.VMEM((3, clips, 4, cols, ch), bf16),
            pltpu.VMEM((clips, cols, ch), bf16),
            pltpu.VMEM((clips, cols, ch), bf16),
            pltpu.VMEM((clips, cols, ch), bf16),
            pltpu.VMEM((clips, 8, ch), f32),
            pltpu.VMEM((clips, 8, ch), f32),
            pltpu.VMEM((9, 3, ch, ch), bf16),
            pltpu.VMEM((ch, 3 * ch), bf16),
            pltpu.VMEM((ch, ch), bf16),
            pltpu.VMEM((clips, 2 * cols, 3 * ch), f32),
            pltpu.VMEM((frames, cols, ch), bf16),
            pltpu.VMEM((frames, cols, ch), bf16),
            pltpu.VMEM((n_rows, per, cols, ch), bf16),
            pltpu.VMEM((n_rows * cols, ch), f32),
            pltpu.VMEM((n_rows * cols, ch), f32),
            pltpu.VMEM((n_rows * cols, ch), bf16),
            pltpu.VMEM((n_rows, per, cols, ch), bf16),
            pltpu.VMEM((frames, cols, ch), bf16),
            dma((9,)),
            dma((2,)),
            dma((6,)),
            dma((6,)),
            dma((4,)),
            dma((4,)),
            dma((n_rows - 1,)),
            dma((n_rows - 1,)),
            dma((n_rows - 1,)),
            dma((n_rows - 1,)),
        ],
        compiler_params=pltpu.CompilerParams(
            collective_id=0, has_side_effects=True, vmem_limit_bytes=56 * 1024 * 1024
        ),
        name="segment",
    )(
        segment_input,
        inner_input,
        lengths.T,
        inner_gain,
        causal_weight,
        causal_bias,
        attention_gain,
        triple_weight,
        triple_bias,
        output_weight,
        output_bias,
    )


def solution(mesh):
    placed = (
        P("clips", "tm", "rows", None, None),
        P("clips", "tm", "rows", None, None),
        P("clips", "tm"),
        P(),
        P(),
        P(),
        P(),
        P(),
        P(),
        P(),
        P(),
    )
    return jax.shard_map(
        functools.partial(segment, mesh.shape["tm"], mesh.shape["rows"]),
        mesh=mesh,
        in_specs=placed,
        out_specs=P("clips", "tm", "rows", None, None),
        check_vma=False,
    )
```

```python
import functools
import math

import jax
import jax.numpy as jnp
from jax import lax
from jax.experimental import pallas as pl
from jax.experimental.pallas import tpu as pltpu
from jax.sharding import PartitionSpec as P

EPSILON = 1e-06


def loop(count, step):
    if count == 1:
        step(0)
    else:

        def one(index, carry):
            step(index)
            return carry

        lax.fori_loop(0, count, one, 0)


def in_three(x):
    high = x.astype(jnp.bfloat16)
    rest = x - high.astype(jnp.float32)
    middle = rest.astype(jnp.bfloat16)
    return high, middle, (rest - middle.astype(jnp.float32)).astype(jnp.bfloat16)


TAPS = ((2, 1), (1, 1), (0, 1), (2, 0), (2, 2), (1, 0), (1, 2), (0, 0), (0, 2))
STAGES = ((0, 1), (1, 3), (3, 5), (5, 7), (7, 9))


def segment_kernel(
    n_tm,
    n_rows,
    clips,
    cols,
    ch,
    seg_any,
    inner_any,
    len_any,
    inner_gain_any,
    weight_ref,
    conv_bias_any,
    attn_gain_any,
    triple_ref,
    triple_bias_any,
    output_ref,
    output_bias_any,
    out_ref,
    seg_ref,
    inner_ref,
    len_ref,
    inner_gain_ref,
    conv_bias_ref,
    attn_gain_ref,
    triple_bias_ref,
    output_bias_ref,
    insem,
    ext,
    prev,
    prev2,
    last,
    flag_out,
    flag_in,
    wbuf,
    tbuf,
    obuf,
    conv,
    residual,
    normed,
    gathered,
    qbuf,
    kbuf,
    vbuf,
    result,
    returned,
    wsem,
    psem,
    near_send,
    near_recv,
    tm_send,
    tm_recv,
    to_send,
    to_recv,
    back_send,
    back_recv,
):
    s = lax.axis_index("tm")
    r = lax.axis_index("rows")
    frames = 2 * clips
    per = frames // n_rows
    chunk = 2 - clips % 2
    halves = 2 if clips % 2 == 0 and n_rows % 2 == 0 else 1
    share = clips // halves
    step = 2 - share % 2
    bf16, f32 = jnp.bfloat16, jnp.float32

    barrier = pltpu.get_barrier_semaphore()
    for k in range(1, n_rows):
        pl.semaphore_signal(
            barrier,
            inc=1,
            device_id={"rows": lax.rem(r + k, n_rows)},
            device_id_type=pl.DeviceIdType.MESH,
        )
    expected = n_rows - 1
    for k in (-2, -1, 1, 2):
        there = jnp.logical_and(s + k >= 0, s + k < n_tm)
        expected = expected + there.astype(jnp.int32)

        @pl.when(there)
        def _():
            pl.semaphore_signal(
                barrier, inc=1, device_id={"tm": s + k}, device_id_type=pl.DeviceIdType.MESH
            )

    small = [
        pltpu.make_async_copy(src, dst, insem.at[i])
        for i, (src, dst) in enumerate(
            (
                (inner_any, inner_ref),
                (inner_gain_any, inner_gain_ref),
                (len_any, len_ref),
                (seg_any, seg_ref),
                (conv_bias_any, conv_bias_ref),
                (attn_gain_any, attn_gain_ref),
                (triple_bias_any, triple_bias_ref),
                (output_bias_any, output_bias_ref),
            )
        )
    ]
    for copy in small:
        copy.start()

    weight_copies = [
        pltpu.make_async_copy(weight_ref.at[kt, kh], wbuf.at[i], wsem.at[i])
        for i, (kt, kh) in enumerate(TAPS)
    ]
    triple_copy = pltpu.make_async_copy(triple_ref, tbuf, psem.at[0])
    output_copy = pltpu.make_async_copy(output_ref, obuf, psem.at[1])
    for copy in weight_copies + [triple_copy, output_copy]:
        copy.start(priority=1)

    for copy in small[:3]:
        copy.wait()
    inner_gain = inner_gain_ref[...].reshape(1, ch)

    for b in range(clips):
        for t in range(2):
            field = inner_ref[b, t, 0].astype(f32)
            mean = jnp.mean(field * field, axis=-1, keepdims=True)
            v = field * lax.rsqrt(mean + EPSILON) * inner_gain
            ext[1, b, 2 + t] = (v / (1.0 + jnp.exp(-v))).astype(bf16)
        count = len_ref[0, b]
        both = count == 2
        first = ext[1, b, 2].astype(f32)
        second = ext[1, b, 3].astype(f32)
        last[b] = jnp.where(both, second, first).astype(bf16)
        flag_out[b] = jnp.full((8, ch), count.astype(f32), f32)

    own, cached = pl.ds(2, 2), pl.ds(0, 2)
    blank = jnp.zeros((clips, 2, cols, ch), bf16)

    @pl.when(r == 0)
    def _():
        ext[0] = jnp.zeros((clips, 4, cols, ch), bf16)

    @pl.when(r == n_rows - 1)
    def _():
        ext[2] = jnp.zeros((clips, 4, cols, ch), bf16)

    @pl.when(s == 0)
    def _():
        ext[1, :, cached] = blank
        prev[...] = jnp.zeros((clips, cols, ch), bf16)
        flag_in[...] = jnp.zeros((clips, 8, ch), f32)

        @pl.when(r > 0)
        def _():
            ext[0, :, cached] = blank

        @pl.when(r < n_rows - 1)
        def _():
            ext[2, :, cached] = blank

    @pl.when(s <= 1)
    def _():
        prev2[...] = jnp.zeros((clips, cols, ch), bf16)

    def remote(src, dst, send, recv, where):
        return pltpu.make_async_remote_copy(
            src_ref=src,
            dst_ref=dst,
            send_sem=send,
            recv_sem=recv,
            device_id=where,
            device_id_type=pl.DeviceIdType.MESH,
        )

    down, up = {"rows": r + 1}, {"rows": r - 1}
    has_down, has_up = r < n_rows - 1, r > 0
    own_down = remote(ext.at[1, :, own], ext.at[0, :, own], near_send.at[0], near_recv.at[0], down)
    own_up = remote(ext.at[1, :, own], ext.at[2, :, own], near_send.at[1], near_recv.at[1], up)
    old_down, old_up = [], []
    for slot in range(2):
        mine = ext.at[1, :, slot]
        i, j = 2 + 2 * slot, 3 + 2 * slot
        old_down.append(remote(mine, ext.at[0, :, slot], near_send.at[i], near_recv.at[i], down))
        old_up.append(remote(mine, ext.at[2, :, slot], near_send.at[j], near_recv.at[j], up))
    after, later = {"tm": s + 1}, {"tm": s + 2}
    to_flag = remote(flag_out, flag_in, tm_send.at[0], tm_recv.at[0], after)
    to_last = remote(last, ext.at[1, :, 1], tm_send.at[1], tm_recv.at[1], after)
    to_first = remote(ext.at[1, :, 2], prev, tm_send.at[2], tm_recv.at[2], after)
    to_after = remote(last, prev2, tm_send.at[3], tm_recv.at[3], later)

    pl.semaphore_wait(barrier, expected)

    @pl.when(s + 1 < n_tm)
    def _():
        to_last.start()
        to_flag.start()
        to_first.start()

    @pl.when(s + 2 < n_tm)
    def _():
        to_after.start()

    @pl.when(has_down)
    def _():
        own_down.start()

    @pl.when(has_up)
    def _():
        own_up.start()


    def taps_dot(stage, at, chunk):
        begin, end = STAGES[stage]
        parts = [
            ext[kh, pl.ds(at * chunk, chunk), kt : kt + 2].reshape(2 * chunk * cols, ch)
            for kt, kh in TAPS[begin:end]
        ]
        columns = [
            jnp.concatenate([wbuf[i, kw] for i in range(begin, end)], axis=0) for kw in range(3)
        ]
        return jnp.dot(
            jnp.concatenate(parts, axis=-1),
            jnp.concatenate(columns, axis=-1),
            preferred_element_type=f32,
        )

    def weights_here(stage):
        for i in range(*STAGES[stage]):
            weight_copies[i].wait()

    def start(at):
        held = taps_dot(0, at, chunk).reshape(chunk, 2 * cols, 3 * ch)
        conv[pl.ds(at * chunk, chunk)] = held

    weights_here(0)
    loop(clips // chunk, start)

    def pass_on(slot):
        @pl.when(has_down)
        def _():
            old_down[slot].start()

        @pl.when(has_up)
        def _():
            old_up[slot].start()

    def passed_on(slot):
        @pl.when(s > 0)
        def _():
            @pl.when(has_up)
            def _():
                old_down[slot].wait_recv()

            @pl.when(has_down)
            def _():
                old_up[slot].wait_recv()

    @pl.when(s > 0)
    def _():
        to_last.wait_recv()
        pass_on(1)
        to_flag.wait_recv()
        to_first.wait_recv()

        @pl.when(s > 1)
        def _():
            to_after.wait_recv()

        for b in range(clips):
            both = flag_in[b, 0:1, :] > 1.5
            older = jnp.where(both, prev[b].astype(f32), prev2[b].astype(f32))
            ext[1, b, 0] = older.astype(bf16)
        pass_on(0)

    weights_here(1)

    def center(at):
        held = taps_dot(1, at, chunk).reshape(chunk, 2 * cols, 3 * ch)
        conv[pl.ds(at * chunk, chunk)] += held

    loop(clips // chunk, center)

    @pl.when(has_up)
    def _():
        own_down.wait_recv()

    @pl.when(has_down)
    def _():
        own_up.wait_recv()

    weights_here(2)

    def beside(at):
        held = taps_dot(2, at, chunk).reshape(chunk, 2 * cols, 3 * ch)
        conv[pl.ds(at * chunk, chunk)] += held

    loop(clips // chunk, beside)
    weights_here(3)
    passed_on(1)

    def nearer(at):
        held = taps_dot(3, at, chunk).reshape(chunk, 2 * cols, 3 * ch)
        conv[pl.ds(at * chunk, chunk)] += held

    loop(clips // chunk, nearer)
    weights_here(4)
    passed_on(0)

    for copy in small[3:]:
        copy.wait()
    conv_bias = conv_bias_ref[...].reshape(1, ch)
    attn_gain = attn_gain_ref[...].reshape(1, ch)
    triple_bias = triple_bias_ref[...].reshape(1, 3 * ch)
    output_bias = output_bias_ref[...].reshape(1, ch)

    def late(at):
        places = 2 * step * cols
        total = conv[pl.ds(at * step, step)].reshape(places, 3 * ch) + taps_dot(4, at, step)
        column = lax.rem(lax.broadcasted_iota(jnp.int32, (places, ch), 0), cols)
        left = pltpu.roll(total[:, :ch], 1, 0)
        right = pltpu.roll(total[:, 2 * ch :], places - 1, 0)
        summed = total[:, ch : 2 * ch] + jnp.where(column == 0, 0.0, left)
        summed = summed + jnp.where(column == cols - 1, 0.0, right)
        summed = summed + conv_bias
        at_frames = pl.ds(at * 2 * step, 2 * step)
        held = residual[at_frames].reshape(places, ch).astype(f32)
        held = (held + summed).astype(bf16)
        residual[at_frames] = held.reshape(2 * step, cols, ch)
        wide = held.astype(f32)
        mean = jnp.mean(wide * wide, axis=-1, keepdims=True)
        wide = (wide * lax.rsqrt(mean + EPSILON) * attn_gain).astype(bf16)
        normed[at_frames] = wide.reshape(2 * step, cols, ch)

    for b in range(clips):
        for t in range(2):
            residual[2 * b + t] = seg_ref[b, t, 0]
    there = []
    for k in range(1, n_rows):
        peer = lax.rem(r + k, n_rows)
        there.append(
            remote(
                normed.at[pl.ds(peer * per, per)],
                gathered.at[r],
                to_send.at[k - 1],
                to_recv.at[k - 1],
                {"rows": peer},
            )
        )
    for g in range(halves):
        first = g * share // step
        loop(share // step, lambda at: late(first + at))
        for k in range(1, n_rows):

            @pl.when(lax.rem(r + k, n_rows) // (n_rows // halves) == g)
            def _():
                there[k - 1].start()

    gathered[r] = normed[pl.ds(r * per, per)]
    triple_copy.wait()
    output_copy.wait()
    for copy in there:
        copy.wait_recv()

    block = n_rows if n_rows % 4 else 4
    group = n_rows if n_rows % 2 else 2 if n_rows == 4 else block
    turns = n_rows // group
    back = []
    for k in range(1, n_rows):
        peer = lax.rem(r + k, n_rows)
        back.append(
            remote(
                result.at[peer],
                returned.at[pl.ds(r * per, per)],
                back_send.at[k - 1],
                back_recv.at[k - 1],
                {"rows": peer},
            )
        )

    for frame in range(per):

        def project(at):
            x = gathered[pl.ds(at * block, block), frame].reshape(block * cols, ch)
            packed = jnp.dot(x, tbuf[...], preferred_element_type=f32) + triple_bias
            rows = pl.ds(at * block * cols, block * cols)
            high, middle, low = in_three(packed[:, :ch])
            qbuf[rows] = jnp.concatenate([high, high, middle, high, middle, low], axis=-1)
            high, middle, low = in_three(packed[:, ch : 2 * ch])
            kbuf[rows] = jnp.concatenate([high, middle, high, low, middle, high], axis=-1)
            vbuf[rows] = packed[:, 2 * ch :].astype(bf16)

        def attend_rows(turn):
            at = lax.rem(r // group + turns // 2 + turn, turns)
            queries = qbuf[pl.ds(at * group * cols, group * cols)]
            scores = lax.dot_general(
                queries, kbuf[...], (((1,), (1,)), ((), ())), preferred_element_type=f32
            ) / math.sqrt(ch)
            exponent = jnp.exp(scores - jnp.max(scores, axis=-1, keepdims=True))
            weights = (exponent / jnp.sum(exponent, axis=-1, keepdims=True)).astype(bf16)
            attended = jnp.dot(weights, vbuf[...], preferred_element_type=f32).astype(bf16)
            projected = jnp.dot(attended, obuf[...], preferred_element_type=f32)
            projected = (projected + output_bias).astype(bf16)
            result[pl.ds(at * group, group), frame] = projected.reshape(group, cols, ch)
            if frame == per - 1:
                for k in range(1, n_rows):

                    @pl.when(lax.rem(r + k, n_rows) // group == at)
                    def _():
                        back[k - 1].start()

        loop(n_rows // block, project)
        if turns <= 2:
            for turn in range(turns):
                attend_rows(turn)
        else:
            loop(turns, attend_rows)

    returned[pl.ds(r * per, per)] = result[r]
    for copy in back:
        copy.wait_recv()

    for b in range(clips):
        count = len_ref[0, b]
        for t in range(2):
            f = 2 * b + t
            live = (count > t).astype(f32)
            summed = residual[f].astype(f32) + returned[f].astype(f32)
            out_ref[b, t, 0] = (summed * live).astype(bf16)

    for copy in there + back:
        copy.wait_send()

    @pl.when(s + 1 < n_tm)
    def _():
        to_flag.wait_send()
        to_last.wait_send()
        to_first.wait_send()

    @pl.when(s + 2 < n_tm)
    def _():
        to_after.wait_send()

    @pl.when(has_down)
    def _():
        own_down.wait_send()

        @pl.when(s > 0)
        def _():
            for copy in old_down:
                copy.wait_send()

    @pl.when(has_up)
    def _():
        own_up.wait_send()

        @pl.when(s > 0)
        def _():
            for copy in old_up:
                copy.wait_send()


def segment(
    n_tm,
    n_rows,
    segment_input,
    inner_input,
    lengths,
    inner_gain,
    causal_weight,
    causal_bias,
    attention_gain,
    triple_weight,
    triple_bias,
    output_weight,
    output_bias,
):
    clips, _, _, cols, ch = segment_input.shape
    frames = 2 * clips
    per = frames // n_rows
    bf16, f32 = jnp.bfloat16, jnp.float32
    vmem = pl.BlockSpec(memory_space=pltpu.VMEM)
    hbm = pl.BlockSpec(memory_space=pl.ANY)
    dma = pltpu.SemaphoreType.DMA
    return pl.pallas_call(
        functools.partial(segment_kernel, n_tm, n_rows, clips, cols, ch),
        out_shape=pltpu.VMEM(segment_input.shape, bf16),
        in_specs=[hbm] * 11,
        out_specs=vmem,
        scratch_shapes=[
            pltpu.VMEM(segment_input.shape, bf16),
            pltpu.VMEM(inner_input.shape, bf16),
            pltpu.SMEM((1, clips), jnp.int32),
            pltpu.VMEM((ch,), f32),
            pltpu.VMEM((ch,), f32),
            pltpu.VMEM((ch,), f32),
            pltpu.VMEM((3 * ch,), f32),
            pltpu.VMEM((ch,), f32),
            dma((8,)),
            pltpu.VMEM((3, clips, 4, cols, ch), bf16),
            pltpu.VMEM((clips, cols, ch), bf16),
            pltpu.VMEM((clips, cols, ch), bf16),
            pltpu.VMEM((clips, cols, ch), bf16),
            pltpu.VMEM((clips, 8, ch), f32),
            pltpu.VMEM((clips, 8, ch), f32),
            pltpu.VMEM((9, 3, ch, ch), bf16),
            pltpu.VMEM((ch, 3 * ch), bf16),
            pltpu.VMEM((ch, ch), bf16),
            pltpu.VMEM((clips, 2 * cols, 3 * ch), f32),
            pltpu.VMEM((frames, cols, ch), bf16),
            pltpu.VMEM((frames, cols, ch), bf16),
            pltpu.VMEM((n_rows, per, cols, ch), bf16),
            pltpu.VMEM((n_rows * cols, 6 * ch), bf16),
            pltpu.VMEM((n_rows * cols, 6 * ch), bf16),
            pltpu.VMEM((n_rows * cols, ch), bf16),
            pltpu.VMEM((n_rows, per, cols, ch), bf16),
            pltpu.VMEM((frames, cols, ch), bf16),
            dma((9,)),
            dma((2,)),
            dma((6,)),
            dma((6,)),
            dma((4,)),
            dma((4,)),
            dma((n_rows - 1,)),
            dma((n_rows - 1,)),
            dma((n_rows - 1,)),
            dma((n_rows - 1,)),
        ],
        compiler_params=pltpu.CompilerParams(
            collective_id=0, has_side_effects=True, vmem_limit_bytes=56 * 1024 * 1024
        ),
        name="segment",
    )(
        segment_input,
        inner_input,
        lengths.T,
        inner_gain,
        causal_weight,
        causal_bias,
        attention_gain,
        triple_weight,
        triple_bias,
        output_weight,
        output_bias,
    )


def solution(mesh):
    placed = (
        P("clips", "tm", "rows", None, None),
        P("clips", "tm", "rows", None, None),
        P("clips", "tm"),
        P(),
        P(),
        P(),
        P(),
        P(),
        P(),
        P(),
        P(),
    )
    return jax.shard_map(
        functools.partial(segment, mesh.shape["tm"], mesh.shape["rows"]),
        mesh=mesh,
        in_specs=placed,
        out_specs=P("clips", "tm", "rows", None, None),
        check_vma=False,
    )
```
